512 devices in a mesh: blk: 32 (over x, z_lo), narrow: 16 (over z_hi, y, core).
Axes of the slice: x: 4, y: 4, z: 16 (z_hi: 2, z_lo: 8; z = z_hi * 8 + z_lo), core: 2. Of those that a mesh axis runs over, the one named last changes fastest.
Arguments:
- queries: bfloat16 [1024, 768], P('blk'), may hold values from -20 to 20
- passages: bfloat16 [524288, 768], P(('blk', 'narrow')), may hold values from -2.1 to 2.1
- positives: int32 [1024], replicated, may hold values from 0 to 524287
Outputs:
- query_loss: float32 [1024], P('blk')
- query_grad: float32 [1024, 768], P('blk')
- passage_grad: float32 [524288, 768], P(('blk', 'narrow'))
The draws below stay inside these ranges and needn't reach their ends.
All inputs are finite; a program needn't handle non-finite values.
Results may differ from the reference program's by a relative error of at most 0.009.
Values may be sent and summed in bfloat16 or wider, within the bound.
No kernel may reach another device: no remote copies, remote signals or barrier semaphores. Data moves between devices by JAX's collectives and lax.ppermute only.
A program may use at most 64 MiB of HBM per device.

```python
import math
import jax
import jax.numpy as jnp
from jax import lax

D = 768
QUERIES = 1024
CORPUS = 524288


def anchor_rows():
    return jnp.arange(8, dtype=jnp.int32) * (CORPUS // 8) + 7


def passage_field(key):
    scale = 3.0 / math.sqrt(D)
    base = jax.random.truncated_normal(jax.random.fold_in(key, 11), -6.0, 6.0, (CORPUS, D), jnp.float32) * scale
    slope = 0.9 + 0.13 * jnp.arange(CORPUS, dtype=jnp.float32) / CORPUS
    field = base * slope[:, None]
    anchors = anchor_rows()
    partners = anchors + CORPUS // 16
    field = field.at[anchors].set(field[anchors])
    field = field.at[partners].set(field[partners])
    return jnp.clip(field, -2.1, 2.1)


def query_field(key):
    key = jax.random.fold_in(key, 5)
    own = jax.random.truncated_normal(jax.random.fold_in(key, 1), -6.0, 6.0, (QUERIES, D), jnp.float32)
    targets = jnp.arange(8, dtype=jnp.int32) * (QUERIES // 8) + 1
    field_rows = own.at[targets].set(own[targets])
    return jnp.clip(field_rows, -20.0, 20.0)


def draw_queries(key, part):
    return query_field(key).astype(jnp.bfloat16)


def draw_passages(key, part):
    return passage_field(key).astype(jnp.bfloat16)


def set_ends(values, own_key, smallest, largest):
    longest = values.shape.index(max(values.shape))
    spots = []
    for shift in (0, 1):
        where = [jax.random.randint(jax.random.fold_in(own_key, axis), (), 0, length) for axis, length in enumerate(values.shape)]
        where[longest] = (where[longest] + shift) % values.shape[longest]
        spots.append(tuple(where))
    return values.at[spots[0]].set(smallest).at[spots[1]].set(largest)


def setup_inputs(seed: int = 0) -> dict:
    key_of = jax.random.split(jax.random.key(seed), 4)
    return {
        "queries": draw_queries(jax.random.fold_in(key_of[3], 71), 0),
        "passages": draw_passages(jax.random.fold_in(key_of[3], 71), 0),
        "positives": set_ends(jax.random.randint(key_of[2], (QUERIES,), 0, CORPUS), jax.random.fold_in(key_of[2], 1), 0, CORPUS - 1).astype(jnp.int32),
    }


def reference(queries, passages, positives):
    width = math.gcd(CORPUS, 8192)
    block_count = CORPUS // width
    blocks = passages.reshape(block_count, width, D)
    block_starts = jnp.arange(block_count, dtype=jnp.int32) * width

    def block_scores(passage_block, block_start):
        scores = jnp.dot(queries, passage_block.T, preferred_element_type=jnp.float32)
        columns = block_start + jnp.arange(width, dtype=jnp.int32)
        matches = positives[:, None] == columns[None, :]
        return scores, matches

    def gather_stats(running, block_item):
        row_top, row_total, positive_score = running
        scores, matches = block_scores(block_item[0], block_item[1])
        new_top = jnp.maximum(row_top, jnp.max(scores, axis=1))
        row_total = row_total * jnp.exp(row_top - new_top) + jnp.sum(jnp.exp(scores - new_top[:, None]), axis=1)
        positive_score = positive_score + jnp.sum(jnp.where(matches, scores, jnp.float32(0.0)), axis=1)
        return (new_top, row_total, positive_score), None

    initial = (jnp.full((QUERIES,), -jnp.inf, jnp.float32), jnp.zeros((QUERIES,), jnp.float32), jnp.zeros((QUERIES,), jnp.float32))
    (row_top, row_total, positive_score), _ = lax.scan(gather_stats, initial, (blocks, block_starts))
    log_total = row_top + jnp.log(row_total)
    query_loss = log_total - positive_score

    def gradients(query_grad, block_item):
        scores, matches = block_scores(block_item[0], block_item[1])
        coefficient = (jnp.exp(scores - log_total[:, None]) - matches.astype(jnp.float32)).astype(jnp.bfloat16)
        query_grad = query_grad + jnp.dot(coefficient, block_item[0], preferred_element_type=jnp.float32)
        block_grad = jnp.dot(coefficient.T, queries, preferred_element_type=jnp.float32)
        return query_grad, block_grad

    query_grad, passage_blocks = lax.scan(gradients, jnp.zeros((QUERIES, D), jnp.float32), (blocks, block_starts))
    return query_loss, query_grad, passage_blocks.reshape(CORPUS, D)
```

```python
import jax
import jax.numpy as jnp
from jax import lax
from jax.sharding import Mesh, PartitionSpec as P

F32 = jnp.float32
BF16 = jnp.bfloat16


def swap(value, axis, offset):
    size = lax.axis_size(axis)
    return lax.ppermute(value, axis, [(i, i ^ offset) for i in range(size)])


def flip_if(bit, value, axis):
    return jnp.where(bit == 1, jnp.flip(value, axis), value)


def relative(value):
    y = lax.axis_index("y")
    value = flip_if(lax.axis_index("c"), value, 0)
    value = flip_if(y // 2, value, 1)
    return flip_if(y % 2, value, 2)


def gather_yc(piece):
    row = jnp.stack([piece] + [swap(piece, "y", k) for k in (1, 2, 3)])
    return jnp.stack([row, swap(row, "c", 1)])


def merge(parts):
    top = jnp.max(parts[:, 0], axis=0)
    total = jnp.sum(parts[:, 1] * jnp.exp(parts[:, 0] - top), axis=0)
    return jnp.stack([top, total, jnp.sum(parts[:, 2], axis=0)])


def body(queries, passages, positives):
    rows, width = queries.shape
    passage_count = passages.shape[0]
    blk = lax.axis_size("blk")
    mine = lax.axis_index("blk")
    y = lax.axis_index("y")
    core = lax.axis_index("c")
    device = ((mine * lax.axis_size("zh") + lax.axis_index("zh")) * 4 + y) * 2 + core
    offset = device * passage_count
    part = rows // 8
    count = blk * rows

    piece = lax.dynamic_slice_in_dim(queries, (y * 2 + core) * part, part)
    column = lax.all_to_all(
        jnp.broadcast_to(piece[None], (blk, part, width)), "blk", 0, 0, tiled=True
    )
    every_query = gather_yc(column).reshape(count, width)

    targets = positives.reshape(blk, 2, 2, 2, part).transpose(3, 1, 2, 0, 4)
    targets = relative(targets).reshape(count)
    columns = offset + lax.iota(jnp.int32, passage_count)
    matches = targets[:, None] == columns[None, :]

    scores = lax.dot_general(
        every_query, passages, (((1,), (1,)), ((), ())), preferred_element_type=F32
    )
    top = jnp.max(scores, axis=1)
    total = jnp.sum(jnp.exp(scores - top[:, None]), axis=1)
    positive = jnp.sum(jnp.where(matches, scores, F32(0.0)), axis=1)

    stats = jnp.stack([top, total, positive]).reshape(3, 2, count // 2)
    other = swap(stats[:, 1], "c", 1)
    stats = merge(jnp.stack([stats[:, 0], other])).reshape(3, 4, blk * part)
    others = [swap(stats[:, k], "y", k) for k in (1, 2, 3)]
    stats = merge(jnp.stack([stats[:, 0]] + others))
    peers = blk * lax.axis_size("zh")
    stats = lax.all_to_all(
        jnp.broadcast_to(stats[None], (peers,) + stats.shape), ("blk", "zh"), 0, 0, tiled=True
    )
    stats = merge(stats)
    log_total = stats[0] + jnp.log(stats[1])
    final = gather_yc(jnp.stack([log_total, log_total - stats[2]]))
    log_totals = final[:, :, 0].reshape(count)
    losses = final[:, :, 1].reshape(2, 2, 2, blk, part)
    losses = lax.dynamic_index_in_dim(losses, mine, 3, keepdims=False)
    query_loss = relative(losses).transpose(1, 2, 0, 3).reshape(rows)

    coefficient = (jnp.exp(scores - log_totals[:, None]) - matches.astype(F32)).astype(BF16)
    partial = jnp.dot(coefficient, passages, preferred_element_type=F32)
    partial = partial.reshape(2, count // 2, width)
    half = partial[0] + swap(partial[1], "c", 1)
    half = half.reshape(4, blk, part, width)
    others = [swap(half[k], "y", k) for k in (1, 2, 3)]
    passage_grad = lax.dot_general(
        coefficient, every_query, (((0,), (0,)), ((), ())), preferred_element_type=F32
    )
    column = half[0] + others[0] + others[1] + others[2]
    column = jnp.sum(lax.all_to_all(column, "blk", 0, 0, tiled=True), axis=0)
    column = column + swap(column, "zh", 1)
    grads = gather_yc(column).reshape(2, 2, 2, part, width)
    query_grad = relative(grads).transpose(1, 2, 0, 3, 4).reshape(rows, width)
    return (query_loss, query_grad, passage_grad)


def solution(mesh):
    blk = mesh.shape["blk"]
    narrow = mesh.shape["narrow"]
    fine = Mesh(mesh.devices.reshape(blk, narrow // 8, 4, 2), ("blk", "zh", "y", "c"))
    every = ("blk", "zh", "y", "c")
    return jax.shard_map(
        body,
        mesh=fine,
        in_specs=(P("blk", None), P(every, None), P()),
        out_specs=(P("blk"), P("blk", None), P(every, None)),
        check_vma=False,
    )
```

```python
import jax
import jax.numpy as jnp
from jax import lax
from jax.sharding import Mesh, PartitionSpec as P

F32 = jnp.float32
BF16 = jnp.bfloat16


def swap(value, axis, offset):
    size = lax.axis_size(axis)
    return lax.ppermute(value, axis, [(i, i ^ offset) for i in range(size)])


def gather_y(piece):
    return [piece] + [swap(piece, "y", k) for k in (1, 2, 3)]


def scatter_y(parts):
    return [parts[0]] + [swap(parts[k], "y", k) for k in (1, 2, 3)]


def flip_if(bit, value, axis):
    return jnp.where(bit == 1, jnp.flip(value, axis), value)


def relative_y(value, axis):
    y = lax.axis_index("y")
    return flip_if(y % 2, flip_if(y // 2, value, axis), axis + 1)


def scores_of(left, right):
    return lax.dot_general(left, right, (((1,), (1,)), ((), ())), preferred_element_type=F32)


def dot(left, right):
    return jnp.dot(left, right, preferred_element_type=F32)


def merge(parts):
    top = jnp.max(parts[:, 0], axis=0)
    total = jnp.sum(parts[:, 1] * jnp.exp(parts[:, 0] - top), axis=0)
    return jnp.stack([top, total, jnp.sum(parts[:, 2], axis=0)])


def body(queries, passages, positives):
    rows, width = queries.shape
    passage_count = passages.shape[0]
    blk = lax.axis_size("blk")
    zh = lax.axis_size("zh")
    mine = lax.axis_index("blk")
    y = lax.axis_index("y")
    core = lax.axis_index("c")
    chip = (mine * zh + lax.axis_index("zh")) * 4 + y
    part = rows // 8
    column = blk * part
    count = 4 * column

    def to_blocks(value):
        value = jnp.broadcast_to(value[:, None], (blk, zh) + value.shape[1:])
        value = value.reshape((blk * zh,) + value.shape[2:])
        return lax.all_to_all(value, ("blk", "zh"), 0, 0, tiled=True)

    near, far = passages, swap(passages, "c", 1)
    near_columns = (chip * 2 + core) * passage_count + lax.iota(jnp.int32, passage_count)
    far_columns = (chip * 2 + 1 - core) * passage_count + lax.iota(jnp.int32, passage_count)

    piece = lax.dynamic_slice_in_dim(queries, (core * 4 + y) * part, part)
    pieces = lax.all_to_all(
        jnp.broadcast_to(piece[None], (blk, part, width)), "blk", 0, 0, tiled=True
    )

    targets = positives.reshape(blk, 2, 2, 2, part).transpose(1, 2, 3, 0, 4)
    targets = relative_y(targets, 1).reshape(2, count)
    targets = flip_if(core, targets, 0)
    near_hot = targets[0][:, None] == near_columns[None, :]
    far_hot = targets[0][:, None] == far_columns[None, :]

    positive_rows = (dot(near_hot.astype(BF16), near) + dot(far_hot.astype(BF16), far)).astype(BF16)
    positive_rows = scatter_y(positive_rows.reshape(4, column, width))
    positive_rows = sum(v.astype(F32) for v in positive_rows).astype(BF16)
    positive_rows = to_blocks(positive_rows.reshape(blk, part, width))
    positive_rows = jnp.sum(positive_rows.astype(F32), axis=0)

    own_queries = jnp.stack(gather_y(pieces)).reshape(count, width)
    every_query = jnp.concatenate([own_queries, swap(own_queries, "c", 1)])

    near_scores = scores_of(own_queries, near)
    far_scores = scores_of(own_queries, far)
    top = jnp.maximum(jnp.max(near_scores, axis=1), jnp.max(far_scores, axis=1))
    near_exp = jnp.exp(near_scores - top[:, None])
    far_exp = jnp.exp(far_scores - top[:, None])
    total = jnp.sum(near_exp, axis=1) + jnp.sum(far_exp, axis=1)
    zero = F32(0.0)
    positive = jnp.sum(jnp.where(near_hot, near_scores, zero), axis=1) + jnp.sum(
        jnp.where(far_hot, far_scores, zero), axis=1
    )
    stats = jnp.stack([top, total, positive]).reshape(3, 4, column)
    grads = dot(jnp.where(near_hot, zero, near_exp).astype(BF16), near) + dot(
        jnp.where(far_hot, zero, far_exp).astype(BF16), far
    )
    grads = grads.astype(BF16).reshape(4, column, width)

    stats = jnp.stack(scatter_y([stats[:, k] for k in range(4)]))
    merged = merge(stats)
    weights = jnp.exp(stats[:, 0] - merged[0])
    grads = scatter_y(grads)
    grads = sum(grads[k].astype(F32) * weights[k][:, None] for k in range(4)).astype(BF16)
    grads = to_blocks(grads.reshape(blk, part, width))

    stats = to_blocks(jnp.broadcast_to(merged[None], (blk, 3, column)))
    merged = merge(stats)
    log_total = merged[0] + jnp.log(merged[1])
    final = jnp.stack([log_total, log_total - merged[2]])
    final = jnp.stack(gather_y(final))
    final = jnp.stack([final, swap(final, "c", 1)])
    log_totals = final[:, :, 0].reshape(2 * count)
    losses = final[:, :, 1].reshape(2, 2, 2, blk, part)
    losses = lax.dynamic_index_in_dim(losses, mine, 3, keepdims=False)
    query_loss = flip_if(core, relative_y(losses, 1), 0).reshape(rows)

    hot = targets.reshape(2 * count)[:, None] == near_columns[None, :]
    scores = scores_of(every_query, passages)
    coefficient = (jnp.exp(scores - log_totals[:, None]) - hot.astype(F32)).astype(BF16)
    passage_grad = lax.dot_general(
        coefficient, every_query, (((0,), (0,)), ((), ())), preferred_element_type=F32
    )

    mine_of = lambda value: lax.dynamic_slice_in_dim(value, mine * part, part, axis=-1)
    scales = jnp.exp(mine_of(stats[:, 0]) - mine_of(merged[0])) / mine_of(merged[1])
    at_positive = jnp.exp(mine_of(merged[2]) - mine_of(log_total)) - F32(1.0)
    at_positive = lax.reduce_precision(at_positive, 8, 7)
    query_rows = jnp.sum(grads.astype(F32) * scales[:, :, None], axis=0)
    query_rows = query_rows + at_positive[:, None] * positive_rows
    query_rows = jnp.stack(gather_y(query_rows))
    query_rows = jnp.stack([query_rows, swap(query_rows, "c", 1)])
    query_rows = query_rows.reshape(2, 2, 2, part, width)
    query_grad = flip_if(core, relative_y(query_rows, 1), 0).reshape(rows, width)
    return (query_loss, query_grad, passage_grad)


def solution(mesh):
    blk = mesh.shape["blk"]
    narrow = mesh.shape["narrow"]
    fine = Mesh(mesh.devices.reshape(blk, narrow // 8, 4, 2), ("blk", "zh", "y", "c"))
    every = ("blk", "zh", "y", "c")
    return jax.shard_map(
        body,
        mesh=fine,
        in_specs=(P("blk", None), P(every, None), P()),
        out_specs=(P("blk"), P("blk", None), P(every, None)),
        check_vma=False,
    )
```

```python
import jax
import jax.numpy as jnp
from jax import lax
from jax.experimental import pallas as pl
from jax.experimental.pallas import tpu as pltpu
from jax.sharding import Mesh, PartitionSpec as P

F32 = jnp.float32
BF16 = jnp.bfloat16
I32 = jnp.int32
EXTRA = 16
VMEM = pl.BlockSpec(memory_space=pltpu.VMEM)
SMEM = pl.BlockSpec(memory_space=pltpu.SMEM)
PARAMS = pltpu.CompilerParams(vmem_limit_bytes=48 * 1024 * 1024)


def swap(value, axis, offset):
    size = lax.axis_size(axis)
    return lax.ppermute(value, axis, [(i, i ^ offset) for i in range(size)])


def gather_y(piece):
    return [piece] + [swap(piece, "y", k) for k in (1, 2, 3)]


def scatter_y(parts):
    return [parts[0]] + [swap(parts[k], "y", k) for k in (1, 2, 3)]


def flip_if(bit, value, axis):
    return jnp.where(bit == 1, jnp.flip(value, axis), value)


def relative_y(value, axis):
    y = lax.axis_index("y")
    return flip_if(y % 2, flip_if(y // 2, value, axis), axis + 1)


def times_t(left, right):
    return lax.dot_general(left, right, (((1,), (1,)), ((), ())), preferred_element_type=F32)


def dot(left, right):
    return jnp.dot(left, right, preferred_element_type=F32)


def split(value):
    high = value.astype(BF16).astype(F32)
    rest = value - high
    middle = rest.astype(BF16).astype(F32)
    return high, middle, rest - middle


def select(index, values):
    out = jnp.zeros_like(index, dtype=F32)
    for i, value in enumerate(values):
        out = jnp.where(index == i, value, out)
    return out


def rows_kernel(offsets, targets, near, far, out):
    columns = lax.broadcasted_iota(I32, (targets.shape[0], near.shape[0]), 1)
    near_hot = (targets[...] - offsets[0] == columns).astype(F32).astype(BF16)
    far_hot = (targets[...] - offsets[1] == columns).astype(F32).astype(BF16)
    out[...] = (dot(near_hot, near[...]) + dot(far_hot, far[...])).astype(BF16)


def positive_rows_of(offsets, targets, near, far):
    return pl.pallas_call(
        rows_kernel,
        out_shape=jax.ShapeDtypeStruct((targets.shape[0], near.shape[1]), BF16),
        in_specs=[SMEM, VMEM, VMEM, VMEM],
        out_specs=VMEM,
        compiler_params=PARAMS,
    )(offsets, targets, near, far)


def parts_kernel(offsets, targets, queries, near, far, out):
    count = queries.shape[0]
    chunk = out.shape[1] - EXTRA
    near_scores = times_t(queries[...], near[...])
    far_scores = times_t(queries[...], far[...])
    columns = lax.broadcasted_iota(I32, near_scores.shape, 1)
    near_hot = targets[...] - offsets[0] == columns
    far_hot = targets[...] - offsets[1] == columns
    top = jnp.max(jnp.maximum(near_scores, far_scores), axis=1, keepdims=True)
    near_exp = jnp.exp(near_scores - top)
    far_exp = jnp.exp(far_scores - top)
    total = jnp.sum(near_exp + far_exp, axis=1, keepdims=True)
    positive = jnp.sum(
        jnp.where(near_hot, near_scores, 0.0) + jnp.where(far_hot, far_scores, 0.0),
        axis=1,
        keepdims=True,
    )
    grads = dot(jnp.where(near_hot, 0.0, near_exp).astype(BF16), near[...])
    grads = grads + dot(jnp.where(far_hot, 0.0, far_exp).astype(BF16), far[...])
    pieces = [v for triple in zip(split(top), split(total), split(positive)) for v in triple]
    stats = select(lax.broadcasted_iota(I32, (count, 128), 1), pieces).T
    for k in range(count // chunk):
        here = slice(k * chunk, (k + 1) * chunk)
        out[k, :chunk, :] = grads[here].astype(BF16)
        out[k, chunk:, :] = jnp.zeros((EXTRA, out.shape[2]), BF16)
        out[k, chunk:, :chunk] = stats[:EXTRA, here].astype(BF16)


def parts_of(offsets, targets, queries, near, far):
    count, width = queries.shape
    chunk = count // 4
    whole = pl.BlockSpec(near.shape, lambda i: (0, 0))
    return pl.pallas_call(
        parts_kernel,
        grid=(2,),
        out_shape=jax.ShapeDtypeStruct((4, chunk + EXTRA, width), BF16),
        in_specs=[
            SMEM,
            pl.BlockSpec((2 * chunk, 1), lambda i: (i, 0)),
            pl.BlockSpec((2 * chunk, width), lambda i: (i, 0)),
            whole,
            whole,
        ],
        out_specs=pl.BlockSpec((2, chunk + EXTRA, width), lambda i: (i, 0, 0)),
        compiler_params=PARAMS,
    )(offsets, targets, queries, near, far)


def unsplit(rows):
    return [rows[i : i + 1] + rows[i + 3 : i + 4] + rows[i + 6 : i + 7] for i in range(3)]


def merge_kernel(*refs):
    *parts, out, out_stats = refs
    chunk = out.shape[0]
    stats = [unsplit(part[chunk:, :chunk].astype(F32)) for part in parts]
    top = stats[0][0]
    for stat in stats[1:]:
        top = jnp.maximum(top, stat[0])
    total = jnp.zeros_like(top)
    positive = jnp.zeros_like(top)
    grads = jnp.zeros(out.shape, F32)
    for part, stat in zip(parts, stats):
        weight = jnp.exp(stat[0] - top)
        total = total + stat[1] * weight
        positive = positive + stat[2]
        column = jnp.broadcast_to(weight, (chunk, chunk)).T[:, :1]
        grads = grads + part[:chunk, :].astype(F32) * column
    out[...] = grads.astype(BF16)
    pieces = [v for triple in zip(split(top), split(total), split(positive)) for v in triple]
    index = lax.broadcasted_iota(I32, (EXTRA, chunk), 0)
    out_stats[...] = select(index, pieces).astype(BF16)


def merge_parts(parts):
    rows, width = parts[0].shape
    chunk = rows - EXTRA
    return pl.pallas_call(
        merge_kernel,
        out_shape=[
            jax.ShapeDtypeStruct((chunk, width), BF16),
            jax.ShapeDtypeStruct((EXTRA, chunk), BF16),
        ],
        in_specs=[VMEM] * len(parts),
        out_specs=[VMEM, VMEM],
        compiler_params=PARAMS,
    )(*parts)


def passages_kernel(offsets, targets, log_totals, passages, own, other, out):
    start = offsets[0] + pl.program_id(0) * passages.shape[0]
    rows = lax.broadcasted_iota(I32, (passages.shape[0], own.shape[0]), 0) + start
    total = None
    for half, queries in enumerate((own, other)):
        here = slice(half, half + 1)
        scores = times_t(passages[...], queries[...])
        hot = (targets[here, :] == rows).astype(F32)
        coefficient = (jnp.exp(scores - log_totals[here, :]) - hot).astype(BF16)
        term = dot(coefficient, queries[...])
        total = term if total is None else total + term
    out[...] = total


def passage_grad_of(offsets, targets, log_totals, passages, own, other):
    count, width = passages.shape
    step = count // 4
    whole = lambda value: pl.BlockSpec(value.shape, lambda i: (0, 0))
    return pl.pallas_call(
        passages_kernel,
        grid=(count // step,),
        out_shape=jax.ShapeDtypeStruct((count, width), F32),
        in_specs=[
            SMEM,
            whole(targets),
            whole(log_totals),
            pl.BlockSpec((step, width), lambda i: (i, 0)),
            whole(own),
            whole(other),
        ],
        out_specs=pl.BlockSpec((step, width), lambda i: (i, 0)),
        compiler_params=PARAMS,
    )(offsets, targets, log_totals, passages, own, other)


def body(queries, passages, positives):
    rows, width = queries.shape
    passage_count = passages.shape[0]
    blk = lax.axis_size("blk")
    zh = lax.axis_size("zh")
    mine = lax.axis_index("blk")
    y = lax.axis_index("y")
    core = lax.axis_index("c")
    chip = (mine * zh + lax.axis_index("zh")) * 4 + y
    part = rows // 8
    column = blk * part
    count = 4 * column

    def to_blocks(value):
        value = jnp.broadcast_to(value[:, None], (blk, zh) + value.shape[1:])
        value = value.reshape((blk * zh,) + value.shape[2:])
        return lax.all_to_all(value, ("blk", "zh"), 0, 0, tiled=True)

    near, far = passages, swap(passages, "c", 1)
    offsets = jnp.stack([chip * 2 + core, chip * 2 + 1 - core]) * passage_count

    piece = lax.dynamic_slice_in_dim(queries, (core * 4 + y) * part, part)
    pieces = lax.all_to_all(
        jnp.broadcast_to(piece[None], (blk, part, width)), "blk", 0, 0, tiled=True
    )

    targets = positives.reshape(blk, 2, 2, 2, part).transpose(1, 2, 3, 0, 4)
    targets = flip_if(core, relative_y(targets, 1).reshape(2, count), 0)
    own_targets = targets[0][:, None]

    positive_rows = positive_rows_of(offsets, own_targets, near, far)
    positive_rows = scatter_y(positive_rows.reshape(4, column, width))
    pieces, positive_rows = lax.optimization_barrier((pieces, positive_rows))
    positive_rows = sum(v.astype(F32) for v in positive_rows).astype(BF16)
    positive_rows = to_blocks(positive_rows.reshape(blk, part, width))

    own_queries = jnp.stack(gather_y(pieces)).reshape(count, width)
    parts = parts_of(offsets, own_targets, own_queries, near, far)
    parts, positive_rows = lax.optimization_barrier((parts, positive_rows))
    positive_rows = jnp.sum(positive_rows.astype(F32), axis=0)
    grads, stats = merge_parts(scatter_y([parts[k] for k in range(4)]))

    lanes = stats[: 2 * width // column].reshape(1, -1, width)
    extra = lanes.shape[1]
    lanes = jnp.broadcast_to(lanes, (blk, extra, width))
    received = to_blocks(jnp.concatenate([grads.reshape(blk, part, width), lanes], axis=1))

    other_queries = swap(own_queries, "c", 1)
    received, other_queries = lax.optimization_barrier((received, other_queries))
    stats = received[:, part:].reshape(blk * zh, -1, column)[:, :9].astype(F32)
    stats = stats.reshape(blk * zh, 3, 3, column).sum(axis=1)
    tops = stats[:, 0]
    top = jnp.max(tops, axis=0)
    weights = jnp.exp(tops - top)
    total = jnp.sum(stats[:, 1] * weights, axis=0)
    positive = jnp.sum(stats[:, 2], axis=0)
    log_total = top + jnp.log(total)
    mine_of = lambda value: lax.dynamic_slice_in_dim(value, mine * part, part, axis=-1)
    scales = mine_of(weights) / mine_of(total)
    at_positive = jnp.exp(mine_of(positive) - mine_of(log_total)) - F32(1.0)
    at_positive = lax.reduce_precision(at_positive, 8, 7)
    query_rows = jnp.sum(received[:, :part].astype(F32) * scales[:, :, None], axis=0)
    query_rows = query_rows + at_positive[:, None] * positive_rows

    final = jnp.concatenate([log_total, log_total - positive])
    final = jnp.pad(final, (0, width - 2 * column))[None]
    final = jnp.stack(gather_y(jnp.concatenate([query_rows, final])))
    final = jnp.stack([final, swap(final, "c", 1)])
    log_totals = final[:, :, part, :column].reshape(2, count)
    passage_grad = passage_grad_of(
        offsets, targets, log_totals, passages, own_queries, other_queries
    )
    losses = final[:, :, part, column : 2 * column].reshape(2, 2, 2, blk, part)
    losses = lax.dynamic_index_in_dim(losses, mine, 3, keepdims=False)
    query_loss = flip_if(core, relative_y(losses, 1), 0).reshape(rows)
    query_rows = final[:, :, :part].reshape(2, 2, 2, part, width)
    query_grad = flip_if(core, relative_y(query_rows, 1), 0).reshape(rows, width)
    return (query_loss, query_grad, passage_grad)


def solution(mesh):
    blk = mesh.shape["blk"]
    narrow = mesh.shape["narrow"]
    fine = Mesh(mesh.devices.reshape(blk, narrow // 8, 4, 2), ("blk", "zh", "y", "c"))
    every = ("blk", "zh", "y", "c")
    return jax.shard_map(
        body,
        mesh=fine,
        in_specs=(P("blk", None), P(every, None), P()),
        out_specs=(P("blk"), P("blk", None), P(every, None)),
        check_vma=False,
    )
```

```python
import jax
import jax.numpy as jnp
from jax import lax
from jax.experimental import pallas as pl
from jax.experimental.pallas import tpu as pltpu
from jax.sharding import Mesh, PartitionSpec as P

F32 = jnp.float32
BF16 = jnp.bfloat16
I32 = jnp.int32
EXTRA = 16
VMEM = pl.BlockSpec(memory_space=pltpu.VMEM)
SMEM = pl.BlockSpec(memory_space=pltpu.SMEM)
PARAMS = pltpu.CompilerParams(vmem_limit_bytes=48 * 1024 * 1024)


def swap(value, axis, offset):
    size = lax.axis_size(axis)
    return lax.ppermute(value, axis, [(i, i ^ offset) for i in range(size)])


def gather_y(piece):
    return [piece] + [swap(piece, "y", k) for k in (1, 2, 3)]


def scatter_y(parts):
    return [parts[0]] + [swap(parts[k], "y", k) for k in (1, 2, 3)]


def flip_if(bit, value, axis):
    return jnp.where(bit == 1, jnp.flip(value, axis), value)


def relative_y(value, axis):
    y = lax.axis_index("y")
    return flip_if(y % 2, flip_if(y // 2, value, axis), axis + 1)


def times_t(left, right):
    return lax.dot_general(left, right, (((1,), (1,)), ((), ())), preferred_element_type=F32)


def dot(left, right):
    return jnp.dot(left, right, preferred_element_type=F32)


def split(value):
    high = value.astype(BF16).astype(F32)
    rest = value - high
    middle = rest.astype(BF16).astype(F32)
    return high, middle, rest - middle


def shift_parts(top):
    high, middle, _ = split(top)
    return high, middle


def select(index, values):
    out = jnp.zeros_like(index, dtype=F32)
    for i, value in enumerate(values):
        out = jnp.where(index == i, value, out)
    return out


def rows_kernel(offsets, targets, near, far, out):
    columns = lax.broadcasted_iota(I32, (targets.shape[0], near.shape[0]), 1)
    near_hot = (targets[...] - offsets[0] == columns).astype(F32).astype(BF16)
    far_hot = (targets[...] - offsets[1] == columns).astype(F32).astype(BF16)
    out[...] = (dot(near_hot, near[...]) + dot(far_hot, far[...])).astype(BF16)


def positive_rows_of(offsets, targets, near, far):
    return pl.pallas_call(
        rows_kernel,
        out_shape=jax.ShapeDtypeStruct((targets.shape[0], near.shape[1]), BF16),
        in_specs=[SMEM, VMEM, VMEM, VMEM],
        out_specs=VMEM,
        compiler_params=PARAMS,
    )(offsets, targets, near, far)


def parts_kernel(offsets, targets, queries, near, far, out):
    count = queries.shape[0]
    chunk = out.shape[1] - EXTRA
    near_scores = times_t(queries[...], near[...])
    far_scores = times_t(queries[...], far[...])
    columns = lax.broadcasted_iota(I32, near_scores.shape, 1)
    near_hot = targets[...] - offsets[0] == columns
    far_hot = targets[...] - offsets[1] == columns
    shift = shift_parts(jnp.max(jnp.maximum(near_scores, far_scores), axis=1, keepdims=True))
    top = shift[0] + shift[1]
    near_exp = jnp.exp(near_scores - top)
    far_exp = jnp.exp(far_scores - top)
    total = jnp.sum(near_exp + far_exp, axis=1, keepdims=True)
    positive = jnp.sum(
        jnp.where(near_hot, near_scores, 0.0) + jnp.where(far_hot, far_scores, 0.0),
        axis=1,
        keepdims=True,
    )
    grads = dot(jnp.where(near_hot, 0.0, near_exp).astype(BF16), near[...])
    grads = grads + dot(jnp.where(far_hot, 0.0, far_exp).astype(BF16), far[...])
    pieces = [*shift, *split(total), *split(positive)]
    stats = select(lax.broadcasted_iota(I32, (count, 128), 1), pieces).T
    for k in range(count // chunk):
        here = slice(k * chunk, (k + 1) * chunk)
        out[k, :chunk, :] = grads[here].astype(BF16)
        out[k, chunk:, :] = jnp.zeros((EXTRA, out.shape[2]), BF16)
        out[k, chunk:, :chunk] = stats[:EXTRA, here].astype(BF16)


def parts_of(offsets, targets, queries, near, far):
    count, width = queries.shape
    chunk = count // 4
    whole = pl.BlockSpec(near.shape, lambda i: (0, 0))
    return pl.pallas_call(
        parts_kernel,
        grid=(2,),
        out_shape=jax.ShapeDtypeStruct((4, chunk + EXTRA, width), BF16),
        in_specs=[
            SMEM,
            pl.BlockSpec((2 * chunk, 1), lambda i: (i, 0)),
            pl.BlockSpec((2 * chunk, width), lambda i: (i, 0)),
            whole,
            whole,
        ],
        out_specs=pl.BlockSpec((2, chunk + EXTRA, width), lambda i: (i, 0, 0)),
        compiler_params=PARAMS,
    )(offsets, targets, queries, near, far)


def unsplit(rows):
    row = [rows[i : i + 1] for i in range(8)]
    return row[0] + row[1], row[2] + row[3] + row[4], row[5] + row[6] + row[7]


def merge_kernel(*refs):
    *parts, out, out_stats = refs
    chunk = out.shape[0]
    stats = [unsplit(part[chunk:, :chunk].astype(F32)) for part in parts]
    top = stats[0][0]
    for stat in stats[1:]:
        top = jnp.maximum(top, stat[0])
    total = jnp.zeros_like(top)
    positive = jnp.zeros_like(top)
    grads = jnp.zeros(out.shape, F32)
    for part, stat in zip(parts, stats):
        weight = jnp.exp(stat[0] - top)
        total = total + stat[1] * weight
        positive = positive + stat[2]
        column = jnp.broadcast_to(weight, (chunk, chunk)).T[:, :1]
        grads = grads + part[:chunk, :].astype(F32) * column
    out[...] = grads.astype(BF16)
    pieces = [*shift_parts(top), *split(total), *split(positive)]
    index = lax.broadcasted_iota(I32, (4, chunk), 0)
    out_stats[:, :chunk] = select(index, pieces[0::2]).astype(BF16)
    out_stats[:, chunk:] = select(index, pieces[1::2]).astype(BF16)


def merge_parts(parts):
    rows, width = parts[0].shape
    chunk = rows - EXTRA
    return pl.pallas_call(
        merge_kernel,
        out_shape=[
            jax.ShapeDtypeStruct((chunk, width), BF16),
            jax.ShapeDtypeStruct((4, 2 * chunk), BF16),
        ],
        in_specs=[VMEM] * len(parts),
        out_specs=[VMEM, VMEM],
        compiler_params=PARAMS,
    )(*parts)


def passages_kernel(offsets, targets, log_totals, passages, own, other, out):
    start = offsets[0] + pl.program_id(0) * passages.shape[0]
    rows = lax.broadcasted_iota(I32, (passages.shape[0], own.shape[0]), 0) + start
    total = None
    for half, queries in enumerate((own, other)):
        here = slice(half, half + 1)
        scores = times_t(passages[...], queries[...])
        hot = (targets[here, :] == rows).astype(F32)
        coefficient = (jnp.exp(scores - log_totals[here, :]) - hot).astype(BF16)
        term = dot(coefficient, queries[...])
        total = term if total is None else total + term
    out[...] = total


def passage_grad_of(offsets, targets, log_totals, passages, own, other):
    count, width = passages.shape
    step = count // 4
    whole = lambda value: pl.BlockSpec(value.shape, lambda i: (0, 0))
    return pl.pallas_call(
        passages_kernel,
        grid=(count // step,),
        out_shape=jax.ShapeDtypeStruct((count, width), F32),
        in_specs=[
            SMEM,
            whole(targets),
            whole(log_totals),
            pl.BlockSpec((step, width), lambda i: (i, 0)),
            whole(own),
            whole(other),
        ],
        out_specs=pl.BlockSpec((step, width), lambda i: (i, 0)),
        compiler_params=PARAMS,
    )(offsets, targets, log_totals, passages, own, other)


def order_kernel(places, near, far, out):
    half = near.shape[1]
    for group in range(near.shape[0]):
        peer = lax.bitwise_xor(places[0], group)
        mine, other = near[peer], far[peer]
        low = jnp.where(places[1] == 0, mine, other)
        top = jnp.where(places[1] == 0, other, mine)
        out[2 * half * group : 2 * half * group + half, :] = low
        out[2 * half * group + half : 2 * half * (group + 1), :] = top


def order_rows(places, near, far):
    groups, half, width = near.shape
    return pl.pallas_call(
        order_kernel,
        out_shape=jax.ShapeDtypeStruct((2 * half * groups, width), F32),
        in_specs=[SMEM, VMEM, VMEM],
        out_specs=VMEM,
        compiler_params=PARAMS,
    )(places, near, far)


def body(queries, passages, positives):
    rows, width = queries.shape
    passage_count = passages.shape[0]
    blk = lax.axis_size("blk")
    zh = lax.axis_size("zh")
    mine = lax.axis_index("blk")
    y = lax.axis_index("y")
    core = lax.axis_index("c")
    high = lax.axis_index("zh")
    chip = (mine * zh + high) * 4 + y
    part = rows // 8
    column = blk * part
    count = 4 * column

    near, far = passages, swap(passages, "c", 1)
    offsets = jnp.stack([chip * 2 + core, chip * 2 + 1 - core]) * passage_count

    piece = lax.dynamic_slice_in_dim(queries, (core * 4 + y) * part, part)
    pieces = lax.all_to_all(
        jnp.broadcast_to(piece[None], (blk, part, width)), "blk", 0, 0, tiled=True
    )

    targets = positives.reshape(blk, 2, 2, 2, part).transpose(1, 2, 3, 0, 4)
    targets = flip_if(core, relative_y(targets, 1).reshape(2, count), 0)
    own_targets = targets[0][:, None]

    positive_rows = positive_rows_of(offsets, own_targets, near, far)
    positive_rows = scatter_y(positive_rows.reshape(4, column, width))
    pieces, positive_rows = lax.optimization_barrier((pieces, positive_rows))
    own_queries = jnp.stack(gather_y(pieces)).reshape(count, width)
    positive_rows = sum(v.astype(F32) for v in positive_rows).astype(BF16)
    parts = parts_of(offsets, own_targets, own_queries, near, far)
    grads, stats = merge_parts(scatter_y([parts[k] for k in range(4)]))

    peers = blk * zh
    half = part // zh
    message = jnp.concatenate(
        [grads.reshape(peers, half, width), positive_rows.reshape(peers, half, width)], axis=1
    )
    message = jnp.concatenate(
        [message, jnp.broadcast_to(stats[None], (peers,) + stats.shape)], axis=2
    )
    received = lax.all_to_all(message, ("blk", "zh"), 0, 0, tiled=True)

    other_queries = swap(own_queries, "c", 1)
    received, other_queries = lax.optimization_barrier((received, other_queries))
    stats = received[:, :, width:].reshape(peers, 8, column).astype(F32)
    shifts = stats[:, 0] + stats[:, 1]
    top = jnp.max(shifts, axis=0)
    weights = jnp.exp(shifts - top)
    total = jnp.sum((stats[:, 2] + stats[:, 3] + stats[:, 4]) * weights, axis=0)
    positive = jnp.sum(stats[:, 5] + stats[:, 6] + stats[:, 7], axis=0)
    log_total = top + jnp.log(total)
    first = mine * part
    slice_of = lambda value, start, size: lax.dynamic_slice_in_dim(value, start, size, axis=-1)
    own = first + high * half
    scales = slice_of(weights, own, half) / slice_of(total, own, half)
    at_positive = jnp.exp(slice_of(positive, own, half) - slice_of(log_total, own, half)) - F32(1.0)
    at_positive = lax.reduce_precision(at_positive, 8, 7)
    query_rows = jnp.sum(received[:, :half, :width].astype(F32) * scales[:, :, None], axis=0)
    positive_rows = jnp.sum(received[:, half : 2 * half, :width].astype(F32), axis=0)
    query_rows = query_rows + at_positive[:, None] * positive_rows

    losses = slice_of(log_total - positive, first, part)
    group = lax.broadcasted_iota(I32, (8, part), 0) == core * 4 + y
    losses = jnp.where(group, losses[None], F32(0.0)).reshape(rows)
    final = jnp.concatenate([log_total, losses])
    final = jnp.pad(final, (0, width - column - rows))[None]
    final = jnp.stack(gather_y(jnp.concatenate([query_rows, final])))
    final = jnp.concatenate([final, swap(final, "c", 1)])
    log_totals = final[:, half, :column].reshape(2, count)
    query_loss = jnp.sum(final[:, half, column : column + rows], axis=0)
    query_rows = final[:, :half]
    far_rows = swap(query_rows, "zh", 1)
    passage_grad = passage_grad_of(
        offsets, targets, log_totals, passages, own_queries, other_queries
    )
    places = jnp.stack([core * 4 + y, high])
    query_grad = order_rows(places, query_rows, far_rows)
    return (query_loss, query_grad, passage_grad)


def solution(mesh):
    blk = mesh.shape["blk"]
    narrow = mesh.shape["narrow"]
    fine = Mesh(mesh.devices.reshape(blk, narrow // 8, 4, 2), ("blk", "zh", "y", "c"))
    every = ("blk", "zh", "y", "c")
    return jax.shard_map(
        body,
        mesh=fine,
        in_specs=(P("blk", None), P(every, None), P()),
        out_specs=(P("blk"), P("blk", None), P(every, None)),
        check_vma=False,
    )
```

```python
import jax
import jax.numpy as jnp
from jax import lax
from jax.experimental import pallas as pl
from jax.experimental.pallas import tpu as pltpu
from jax.sharding import Mesh, PartitionSpec as P

F32 = jnp.float32
BF16 = jnp.bfloat16
I32 = jnp.int32
EXTRA = 16
VMEM = pl.BlockSpec(memory_space=pltpu.VMEM)
SMEM = pl.BlockSpec(memory_space=pltpu.SMEM)
PARAMS = pltpu.CompilerParams(vmem_limit_bytes=48 * 1024 * 1024)


def swap(value, axis, offset):
    size = lax.axis_size(axis)
    return lax.ppermute(value, axis, [(i, i ^ offset) for i in range(size)])


def gather(piece, axes):
    size = lax.axis_size(axes)
    return lax.all_to_all(jnp.broadcast_to(piece[None], (size,) + piece.shape), axes, 0, 0, tiled=True)


def times_t(left, right):
    return lax.dot_general(left, right, (((1,), (1,)), ((), ())), preferred_element_type=F32)


def dot(left, right):
    return jnp.dot(left, right, preferred_element_type=F32)


def split(value):
    high = value.astype(BF16).astype(F32)
    rest = value - high
    middle = rest.astype(BF16).astype(F32)
    return high, middle, rest - middle


def shift_parts(top):
    high, middle, _ = split(top)
    return high, middle


def select(index, values):
    out = jnp.zeros_like(index, dtype=F32)
    for i, value in enumerate(values):
        out = jnp.where(index == i, value, out)
    return out


def rows_kernel(offsets, targets, near, far, out):
    columns = lax.broadcasted_iota(I32, (targets.shape[0], near.shape[0]), 1)
    near_hot = (targets[...] - offsets[0] == columns).astype(F32).astype(BF16)
    far_hot = (targets[...] - offsets[1] == columns).astype(F32).astype(BF16)
    out[...] = (dot(near_hot, near[...]) + dot(far_hot, far[...])).astype(BF16)


def positive_rows_of(offsets, targets, near, far):
    return pl.pallas_call(
        rows_kernel,
        out_shape=jax.ShapeDtypeStruct((targets.shape[0], near.shape[1]), BF16),
        in_specs=[SMEM, VMEM, VMEM, VMEM],
        out_specs=VMEM,
        compiler_params=PARAMS,
    )(offsets, targets, near, far)


def parts_kernel(offsets, targets, queries, near, far, out):
    count = queries.shape[0]
    chunk = out.shape[1] - EXTRA
    near_scores = times_t(queries[...], near[...])
    far_scores = times_t(queries[...], far[...])
    columns = lax.broadcasted_iota(I32, near_scores.shape, 1)
    near_hot = targets[...] - offsets[0] == columns
    far_hot = targets[...] - offsets[1] == columns
    shift = shift_parts(jnp.max(jnp.maximum(near_scores, far_scores), axis=1, keepdims=True))
    top = shift[0] + shift[1]
    near_exp = jnp.exp(near_scores - top)
    far_exp = jnp.exp(far_scores - top)
    total = jnp.sum(near_exp + far_exp, axis=1, keepdims=True)
    positive = jnp.sum(
        jnp.where(near_hot, near_scores, 0.0) + jnp.where(far_hot, far_scores, 0.0),
        axis=1,
        keepdims=True,
    )
    grads = dot(jnp.where(near_hot, 0.0, near_exp).astype(BF16), near[...])
    grads = grads + dot(jnp.where(far_hot, 0.0, far_exp).astype(BF16), far[...])
    pieces = [*shift, *split(total), *split(positive)]
    stats = select(lax.broadcasted_iota(I32, (count, 128), 1), pieces).T
    for k in range(count // chunk):
        here = slice(k * chunk, (k + 1) * chunk)
        out[k, :chunk, :] = grads[here].astype(BF16)
        out[k, chunk:, :] = jnp.zeros((EXTRA, out.shape[2]), BF16)
        out[k, chunk:, :chunk] = stats[:EXTRA, here].astype(BF16)


def parts_of(offsets, targets, queries, near, far):
    count, width = queries.shape
    chunk = count // 4
    whole = pl.BlockSpec(near.shape, lambda i: (0, 0))
    return pl.pallas_call(
        parts_kernel,
        grid=(2,),
        out_shape=jax.ShapeDtypeStruct((4, chunk + EXTRA, width), BF16),
        in_specs=[
            SMEM,
            pl.BlockSpec((2 * chunk, 1), lambda i: (i, 0)),
            pl.BlockSpec((2 * chunk, width), lambda i: (i, 0)),
            whole,
            whole,
        ],
        out_specs=pl.BlockSpec((2, chunk + EXTRA, width), lambda i: (i, 0, 0)),
        compiler_params=PARAMS,
    )(offsets, targets, queries, near, far)


def unsplit(rows):
    row = [rows[i : i + 1] for i in range(8)]
    return row[0] + row[1], row[2] + row[3] + row[4], row[5] + row[6] + row[7]


def merge_kernel(messages, out, out_stats):
    chunk = out.shape[0]
    parts = [messages.at[k] for k in range(messages.shape[0])]
    stats = [unsplit(part[chunk:, :chunk].astype(F32)) for part in parts]
    top = stats[0][0]
    for stat in stats[1:]:
        top = jnp.maximum(top, stat[0])
    total = jnp.zeros_like(top)
    positive = jnp.zeros_like(top)
    grads = jnp.zeros(out.shape, F32)
    for part, stat in zip(parts, stats):
        weight = jnp.exp(stat[0] - top)
        total = total + stat[1] * weight
        positive = positive + stat[2]
        column = jnp.broadcast_to(weight, (chunk, chunk)).T[:, :1]
        grads = grads + part[:chunk, :].astype(F32) * column
    out[...] = grads.astype(BF16)
    pieces = [*shift_parts(top), *split(total), *split(positive)]
    index = lax.broadcasted_iota(I32, (4, chunk), 0)
    out_stats[:, :chunk] = select(index, pieces[0::2]).astype(BF16)
    out_stats[:, chunk:] = select(index, pieces[1::2]).astype(BF16)


def merge_parts(messages):
    _, rows, width = messages.shape
    chunk = rows - EXTRA
    return pl.pallas_call(
        merge_kernel,
        out_shape=[
            jax.ShapeDtypeStruct((chunk, width), BF16),
            jax.ShapeDtypeStruct((4, 2 * chunk), BF16),
        ],
        in_specs=[VMEM],
        out_specs=[VMEM, VMEM],
        compiler_params=PARAMS,
    )(messages)


def passages_kernel(offsets, core, targets, log_totals, passages, own, other, out):
    start = offsets[0] + pl.program_id(0) * passages.shape[0]
    rows = lax.broadcasted_iota(I32, (passages.shape[0], own.shape[0]), 0) + start
    total = None
    for half, queries in enumerate((own, other)):
        first = lax.bitwise_xor(core[0], half) * 4
        row_of = lambda ref: jnp.concatenate([ref[pl.ds(first + k, 1), :] for k in range(4)], axis=1)
        scores = times_t(passages[...], queries[...])
        hot = (row_of(targets) == rows).astype(F32)
        coefficient = (jnp.exp(scores - row_of(log_totals)) - hot).astype(BF16)
        term = dot(coefficient, queries[...])
        total = term if total is None else total + term
    out[...] = total


def passage_grad_of(offsets, core, targets, log_totals, passages, own, other):
    count, width = passages.shape
    step = count // 4
    whole = lambda value: pl.BlockSpec(value.shape, lambda i: (0, 0))
    return pl.pallas_call(
        passages_kernel,
        grid=(count // step,),
        out_shape=jax.ShapeDtypeStruct((count, width), F32),
        in_specs=[
            SMEM,
            SMEM,
            whole(targets),
            whole(log_totals),
            pl.BlockSpec((step, width), lambda i: (i, 0)),
            whole(own),
            whole(other),
        ],
        out_specs=pl.BlockSpec((step, width), lambda i: (i, 0)),
        compiler_params=PARAMS,
    )(offsets, core, targets, log_totals, passages, own, other)


def order_kernel(high, near, far, out):
    half = near.shape[1]
    for group in range(near.shape[0]):
        mine, other = near[group], far[group]
        low = jnp.where(high[0] == 0, mine, other)
        top = jnp.where(high[0] == 0, other, mine)
        out[2 * half * group : 2 * half * group + half, :] = low
        out[2 * half * group + half : 2 * half * (group + 1), :] = top


def order_rows(high, near, far):
    groups, half, width = near.shape
    return pl.pallas_call(
        order_kernel,
        out_shape=jax.ShapeDtypeStruct((2 * half * groups, width), F32),
        in_specs=[SMEM, VMEM, VMEM],
        out_specs=VMEM,
        compiler_params=PARAMS,
    )(high, near, far)


def body(queries, passages, positives):
    rows, width = queries.shape
    passage_count = passages.shape[0]
    blk = lax.axis_size("blk")
    zh = lax.axis_size("zh")
    mine = lax.axis_index("blk")
    y = lax.axis_index("y")
    core = lax.axis_index("c")
    high = lax.axis_index("zh")
    chip = (mine * zh + high) * 4 + y
    part = rows // 8
    column = blk * part
    count = 4 * column

    near, far = passages, swap(passages, "c", 1)
    offsets = jnp.stack([chip * 2 + core, chip * 2 + 1 - core]) * passage_count

    pieces = gather(lax.dynamic_slice_in_dim(queries, (core * 4 + y) * part, part), "blk")

    targets = positives.reshape(blk, 8, part).transpose(1, 0, 2).reshape(8, column)
    own_targets = lax.dynamic_slice_in_dim(targets, core * 4, 4).reshape(count, 1)

    positive_rows = positive_rows_of(offsets, own_targets, near, far).reshape(4, column, width)
    pick = lambda k: lax.dynamic_index_in_dim(positive_rows, lax.bitwise_xor(y, k), 0, keepdims=False)
    positive_rows = [pick(0)] + [swap(pick(k), "y", k) for k in (1, 2, 3)]
    pieces, positive_rows = lax.optimization_barrier((pieces, positive_rows))
    own_queries = gather(pieces, "y").reshape(count, width)
    positive_rows = sum(v.astype(F32) for v in positive_rows).astype(BF16)
    parts = parts_of(offsets, own_targets, own_queries, near, far)
    grads, stats = merge_parts(lax.all_to_all(parts, "y", 0, 0, tiled=True))

    peers = blk * zh
    half = part // zh
    message = jnp.concatenate(
        [grads.reshape(peers, half, width), positive_rows.reshape(peers, half, width)], axis=1
    )
    message = jnp.concatenate(
        [message, jnp.broadcast_to(stats[None], (peers,) + stats.shape)], axis=2
    )
    received = lax.all_to_all(message, ("blk", "zh"), 0, 0, tiled=True)

    other_queries = swap(own_queries, "c", 1)
    received, other_queries = lax.optimization_barrier((received, other_queries))
    stats = received[:, :, width:].reshape(peers, 8, column).astype(F32)
    shifts = stats[:, 0] + stats[:, 1]
    top = jnp.max(shifts, axis=0)
    weights = jnp.exp(shifts - top)
    total = jnp.sum((stats[:, 2] + stats[:, 3] + stats[:, 4]) * weights, axis=0)
    positive = jnp.sum(stats[:, 5] + stats[:, 6] + stats[:, 7], axis=0)
    log_total = top + jnp.log(total)
    first = mine * part
    slice_of = lambda value, start, size: lax.dynamic_slice_in_dim(value, start, size, axis=-1)
    own = first + high * half
    scales = slice_of(weights, own, half) / slice_of(total, own, half)
    at_positive = jnp.exp(slice_of(positive, own, half) - slice_of(log_total, own, half)) - F32(1.0)
    at_positive = lax.reduce_precision(at_positive, 8, 7)
    query_rows = jnp.sum(received[:, :half, :width].astype(F32) * scales[:, :, None], axis=0)
    positive_rows = jnp.sum(received[:, half : 2 * half, :width].astype(F32), axis=0)
    query_rows = query_rows + at_positive[:, None] * positive_rows

    losses = slice_of(log_total - positive, first, part)
    final = jnp.concatenate([log_total, losses])
    final = jnp.pad(final, (0, width - column - part))[None]
    final = gather(jnp.concatenate([query_rows, final]), ("c", "y"))
    log_totals = final[:, half, :column]
    query_loss = final[:, half, column : column + part].reshape(rows)
    query_rows = final[:, :half]
    far_rows = swap(query_rows, "zh", 1)
    passage_grad = passage_grad_of(
        offsets, core[None], targets, log_totals, passages, own_queries, other_queries
    )
    query_grad = order_rows(high[None], query_rows, far_rows)
    return (query_loss, query_grad, passage_grad)


def solution(mesh):
    blk = mesh.shape["blk"]
    narrow = mesh.shape["narrow"]
    fine = Mesh(mesh.devices.reshape(blk, narrow // 8, 4, 2), ("blk", "zh", "y", "c"))
    every = ("blk", "zh", "y", "c")
    return jax.shard_map(
        body,
        mesh=fine,
        in_specs=(P("blk", None), P(every, None), P()),
        out_specs=(P("blk"), P("blk", None), P(every, None)),
        check_vma=False,
    )
```

```python
import jax
import jax.numpy as jnp
from jax import lax
from jax.experimental import pallas as pl
from jax.experimental.pallas import tpu as pltpu
from jax.sharding import Mesh, PartitionSpec as P

F32 = jnp.float32
BF16 = jnp.bfloat16
I32 = jnp.int32
EXTRA = 16
VMEM = pl.BlockSpec(memory_space=pltpu.VMEM)
SMEM = pl.BlockSpec(memory_space=pltpu.SMEM)
PARAMS = pltpu.CompilerParams(vmem_limit_bytes=28 * 1024 * 1024)


def swap(value, axis, offset):
    size = lax.axis_size(axis)
    return lax.ppermute(value, axis, [(i, i ^ offset) for i in range(size)])


def gather(piece, axes):
    size = lax.axis_size(axes)
    return lax.all_to_all(jnp.broadcast_to(piece[None], (size,) + piece.shape), axes, 0, 0, tiled=True)


def times_t(left, right):
    return lax.dot_general(left, right, (((1,), (1,)), ((), ())), preferred_element_type=F32)


def dot(left, right):
    return jnp.dot(left, right, preferred_element_type=F32)


def split(value):
    high = value.astype(BF16).astype(F32)
    rest = value - high
    middle = rest.astype(BF16).astype(F32)
    return high, middle, rest - middle


def select(index, values):
    out = jnp.zeros_like(index, dtype=F32)
    for i, value in enumerate(values):
        out = jnp.where(index == i, value, out)
    return out


def rows_kernel(offsets, targets, near, far, out):
    columns = lax.broadcasted_iota(I32, (targets.shape[0], near.shape[0]), 1)
    near_hot = (targets[...] - offsets[0] == columns).astype(F32).astype(BF16)
    far_hot = (targets[...] - offsets[1] == columns).astype(F32).astype(BF16)
    out[...] = (dot(near_hot, near[...]) + dot(far_hot, far[...])).astype(BF16)


def positive_rows_of(offsets, targets, near, far):
    return pl.pallas_call(
        rows_kernel,
        out_shape=jax.ShapeDtypeStruct((targets.shape[0], near.shape[1]), BF16),
        in_specs=[SMEM, VMEM, VMEM, VMEM],
        out_specs=VMEM,
        compiler_params=PARAMS,
    )(offsets, targets, near, far)


def parts_kernel(offsets, targets, queries, near, far, out):
    count = queries.shape[0]
    chunk = out.shape[1] - EXTRA
    near_scores = times_t(queries[...], near[...])
    far_scores = times_t(queries[...], far[...])
    columns = lax.broadcasted_iota(I32, near_scores.shape, 1)
    near_hot = targets[...] - offsets[0] == columns
    far_hot = targets[...] - offsets[1] == columns
    top = jnp.max(jnp.maximum(near_scores, far_scores), axis=1, keepdims=True)
    near_exp = jnp.exp(near_scores - top)
    far_exp = jnp.exp(far_scores - top)
    total = jnp.sum(near_exp + far_exp, axis=1, keepdims=True)
    positive = jnp.sum(
        jnp.where(near_hot, near_scores, 0.0) + jnp.where(far_hot, far_scores, 0.0),
        axis=1,
        keepdims=True,
    )
    grads = dot(jnp.where(near_hot, 0.0, near_exp).astype(BF16), near[...])
    grads = grads + dot(jnp.where(far_hot, 0.0, far_exp).astype(BF16), far[...])
    grads = (grads * (1.0 / total)).astype(BF16)
    pieces = [*split(top + jnp.log(total)), *split(positive)]
    stats = select(lax.broadcasted_iota(I32, (count, 128), 1), pieces).T
    for k in range(count // chunk):
        here = slice(k * chunk, (k + 1) * chunk)
        out[k, :chunk, :] = grads[here]
        out[k, chunk:, :] = jnp.zeros((EXTRA, out.shape[2]), BF16)
        out[k, chunk:, :chunk] = stats[:EXTRA, here].astype(BF16)


def parts_of(offsets, targets, queries, near, far):
    count, width = queries.shape
    return pl.pallas_call(
        parts_kernel,
        out_shape=jax.ShapeDtypeStruct((4, count // 4 + EXTRA, width), BF16),
        in_specs=[SMEM, VMEM, VMEM, VMEM, VMEM],
        out_specs=VMEM,
        compiler_params=PARAMS,
    )(offsets, targets, queries, near, far)


def merge_kernel(messages, out, out_logs, out_positive):
    chunk = out.shape[0]
    peers = out_positive.shape[0]
    parts = [messages.at[k] for k in range(messages.shape[0])]
    stats = [part[chunk:, :chunk].astype(F32) for part in parts]
    logs = [stat[0:1] + stat[1:2] + stat[2:3] for stat in stats]
    positive = sum(stat[3:4] + stat[4:5] + stat[5:6] for stat in stats)
    top = logs[0]
    for log in logs[1:]:
        top = jnp.maximum(top, log)
    weights = [jnp.exp(log - top) for log in logs]
    total = sum(weights)
    grads = jnp.zeros(out.shape, F32)
    for part, weight in zip(parts, weights):
        column = jnp.broadcast_to(weight / total, (chunk, chunk)).T[:, :1]
        grads = grads + part[:chunk, :].astype(F32) * column
    out[...] = grads.astype(BF16)
    index = lax.broadcasted_iota(I32, out_logs.shape, 0)
    out_logs[...] = select(index, split(top + jnp.log(total))).astype(BF16)
    peer = lax.broadcasted_iota(I32, (peers, chunk), 0)
    lane = lax.broadcasted_iota(I32, (peers, chunk), 1)
    each = chunk // peers
    own = jnp.zeros((peers, chunk), F32)
    for row in range(each):
        here = lane == peer * each + row
        value = jnp.sum(jnp.where(here, positive, 0.0), axis=1, keepdims=True)
        for k, piece in enumerate(split(value)):
            own = jnp.where(lane == 3 * row + k, piece, own)
    out_positive[...] = own.astype(BF16)


def merge_parts(messages, peers):
    _, rows, width = messages.shape
    chunk = rows - EXTRA
    return pl.pallas_call(
        merge_kernel,
        out_shape=[
            jax.ShapeDtypeStruct((chunk, width), BF16),
            jax.ShapeDtypeStruct((3, chunk), BF16),
            jax.ShapeDtypeStruct((peers, chunk), BF16),
        ],
        in_specs=[VMEM],
        out_specs=[VMEM, VMEM, VMEM],
        compiler_params=PARAMS,
    )(messages)


def passages_kernel(offsets, core, targets, log_totals, passages, own, other, out):
    start = offsets[0] + pl.program_id(0) * passages.shape[0]
    rows = lax.broadcasted_iota(I32, (passages.shape[0], own.shape[0]), 0) + start
    total = None
    for half, queries in enumerate((own, other)):
        first = lax.bitwise_xor(core[0], half) * 4
        row_of = lambda ref: jnp.concatenate([ref[pl.ds(first + k, 1), :] for k in range(4)], axis=1)
        scores = times_t(passages[...], queries[...])
        hot = (row_of(targets) == rows).astype(F32)
        coefficient = (jnp.exp(scores - row_of(log_totals)) - hot).astype(BF16)
        term = dot(coefficient, queries[...])
        total = term if total is None else total + term
    out[...] = total


def passage_grad_of(offsets, core, targets, log_totals, passages, own, other):
    count, width = passages.shape
    step = count // 2
    return pl.pallas_call(
        passages_kernel,
        grid=(count // step,),
        out_shape=jax.ShapeDtypeStruct((count, width), F32),
        in_specs=[
            SMEM,
            SMEM,
            VMEM,
            VMEM,
            pl.BlockSpec((step, width), lambda i: (i, 0)),
            VMEM,
            VMEM,
        ],
        out_specs=pl.BlockSpec((step, width), lambda i: (i, 0)),
        compiler_params=PARAMS,
        cost_estimate=pl.CostEstimate(
            flops=8 * count * own.shape[0] * width,
            bytes_accessed=10 * count * width,
            transcendentals=2 * count * own.shape[0],
        ),
    )(offsets, core, targets, log_totals, passages, own, other)


def order_kernel(high, near, far, out):
    half = out.shape[0] // (2 * near.shape[0])
    for group in range(near.shape[0]):
        mine, other = near[group, :half], far[group, :half]
        low = jnp.where(high[0] == 0, mine, other)
        top = jnp.where(high[0] == 0, other, mine)
        out[2 * half * group : 2 * half * group + half, :] = low
        out[2 * half * group + half : 2 * half * (group + 1), :] = top


def order_rows(high, near, far, half):
    groups, _, width = near.shape
    return pl.pallas_call(
        order_kernel,
        out_shape=jax.ShapeDtypeStruct((2 * half * groups, width), F32),
        in_specs=[SMEM, VMEM, VMEM],
        out_specs=VMEM,
        compiler_params=PARAMS,
    )(high, near, far)


def body(queries, passages, positives):
    rows, width = queries.shape
    passage_count = passages.shape[0]
    blk = lax.axis_size("blk")
    zh = lax.axis_size("zh")
    mine = lax.axis_index("blk")
    y = lax.axis_index("y")
    core = lax.axis_index("c")
    high = lax.axis_index("zh")
    chip = (mine * zh + high) * 4 + y
    part = rows // 8
    column = blk * part
    count = 4 * column

    near, far = passages, swap(passages, "c", 1)
    offsets = jnp.stack([chip * 2 + core, chip * 2 + 1 - core]) * passage_count

    pieces = gather(lax.dynamic_slice_in_dim(queries, (core * 4 + y) * part, part), "blk")

    targets = positives.reshape(blk, 8, part).transpose(1, 0, 2).reshape(8, column)
    own_targets = lax.dynamic_slice_in_dim(targets, core * 4, 4).reshape(count, 1)

    positive_rows = positive_rows_of(offsets, own_targets, near, far).reshape(4, column, width)
    pieces, positive_rows = lax.optimization_barrier((pieces, positive_rows))
    pick = lambda k: lax.dynamic_index_in_dim(positive_rows, lax.bitwise_xor(y, k), 0, keepdims=False)
    positive_parts = [pick(0)] + [swap(pick(k), "y", k) for k in (1, 2, 3)]
    own_queries = gather(pieces, "y").reshape(count, width)
    own_queries, positive_parts = lax.optimization_barrier((own_queries, positive_parts))
    positive_rows = sum(v.astype(F32) for v in positive_parts).astype(BF16)
    parts = parts_of(offsets, own_targets, own_queries, near, far)
    peers = blk * zh
    half = part // zh
    grads, logs, positive = merge_parts(lax.all_to_all(parts, "y", 0, 0, tiled=True), peers)

    message = jnp.concatenate(
        [grads.reshape(peers, half, width), positive_rows.reshape(peers, half, width)], axis=1
    )
    logs = jnp.broadcast_to(logs[None], (peers,) + logs.shape)
    extra = jnp.concatenate([logs, positive[:, None]], axis=1)
    received = lax.all_to_all(
        jnp.concatenate([message, extra], axis=2), ("blk", "zh"), 0, 0, tiled=True
    )

    other_queries = swap(own_queries, "c", 1)
    received, other_queries = lax.optimization_barrier((received, other_queries))
    logs = jnp.sum(received[:, :3, width:].astype(F32), axis=1)
    top = jnp.max(logs, axis=0)
    weights = jnp.exp(logs - top)
    total = jnp.sum(weights, axis=0)
    log_total = top + jnp.log(total)
    positive = received[:, 3, width : width + 3 * half].astype(F32)
    positive = jnp.sum(positive.reshape(peers, half, 3), axis=(0, 2))
    own = mine * part + high * half
    own_of = lambda value: lax.dynamic_slice_in_dim(value, own, half, axis=-1)
    scales = own_of(weights) / own_of(total)
    at_positive = jnp.exp(positive - own_of(log_total)) - F32(1.0)
    at_positive = lax.reduce_precision(at_positive, 8, 7)
    query_rows = jnp.sum(received[:, :half, :width].astype(F32) * scales[:, :, None], axis=0)
    positive_rows = jnp.sum(received[:, half:, :width].astype(F32), axis=0)
    query_rows = query_rows + at_positive[:, None] * positive_rows

    losses = own_of(log_total) - positive
    final = jnp.pad(log_total, (0, width - column))
    place = column + (core * 4 + y) * part + high * half
    final = lax.dynamic_update_slice_in_dim(final, losses, place, 0)
    final = gather(jnp.concatenate([query_rows, final[None]]), ("c", "y"))
    final = lax.optimization_barrier(final)
    far_final = swap(final, "zh", 1)
    log_totals = final[:, half, :column]
    passage_grad = passage_grad_of(
        offsets, core[None], targets, log_totals, passages, own_queries, other_queries
    )
    losses_of = lambda value: jnp.sum(value[:, half, column : column + rows], axis=0)
    query_loss = losses_of(final) + losses_of(far_final)
    query_grad = order_rows(high[None], final, far_final, half)
    return (query_loss, query_grad, passage_grad)


def solution(mesh):
    blk = mesh.shape["blk"]
    narrow = mesh.shape["narrow"]
    fine = Mesh(mesh.devices.reshape(blk, narrow // 8, 4, 2), ("blk", "zh", "y", "c"))
    every = ("blk", "zh", "y", "c")
    return jax.shard_map(
        body,
        mesh=fine,
        in_specs=(P("blk", None), P(every, None), P()),
        out_specs=(P("blk"), P("blk", None), P(every, None)),
        check_vma=False,
    )
```

```python
import jax
import jax.numpy as jnp
from jax import lax
from jax.experimental import pallas as pl
from jax.experimental.pallas import tpu as pltpu
from jax.sharding import Mesh, PartitionSpec as P

F32 = jnp.float32
BF16 = jnp.bfloat16
I32 = jnp.int32
EXTRA = 16
VMEM = pl.BlockSpec(memory_space=pltpu.VMEM)
SMEM = pl.BlockSpec(memory_space=pltpu.SMEM)
PARAMS = pltpu.CompilerParams(vmem_limit_bytes=28 * 1024 * 1024)


def swap(value, axis, offset):
    size = lax.axis_size(axis)
    return lax.ppermute(value, axis, [(i, i ^ offset) for i in range(size)])


def gather(piece, axes):
    size = lax.axis_size(axes)
    return lax.all_to_all(jnp.broadcast_to(piece[None], (size,) + piece.shape), axes, 0, 0, tiled=True)


def times_t(left, right):
    return lax.dot_general(left, right, (((1,), (1,)), ((), ())), preferred_element_type=F32)


def dot(left, right):
    return jnp.dot(left, right, preferred_element_type=F32)


def split(value):
    high = value.astype(BF16).astype(F32)
    rest = value - high
    middle = rest.astype(BF16).astype(F32)
    return high, middle, rest - middle


def select(index, values):
    out = jnp.zeros_like(index, dtype=F32)
    for i, value in enumerate(values):
        out = jnp.where(index == i, value, out)
    return out


def rows_kernel(offsets, targets, near, far, out):
    columns = lax.broadcasted_iota(I32, (targets.shape[0], near.shape[0]), 1)
    near_hot = (targets[...] - offsets[0] == columns).astype(F32).astype(BF16)
    far_hot = (targets[...] - offsets[1] == columns).astype(F32).astype(BF16)
    out[...] = (dot(near_hot, near[...]) + dot(far_hot, far[...])).astype(BF16)


def positive_rows_of(offsets, targets, near, far):
    return pl.pallas_call(
        rows_kernel,
        out_shape=jax.ShapeDtypeStruct((targets.shape[0], near.shape[1]), BF16),
        in_specs=[SMEM, VMEM, VMEM, VMEM],
        out_specs=VMEM,
        compiler_params=PARAMS,
    )(offsets, targets, near, far)


def parts_kernel(offsets, targets, queries, near, far, out):
    count = queries.shape[0]
    chunk = out.shape[1] - EXTRA
    near_scores = times_t(queries[...], near[...])
    far_scores = times_t(queries[...], far[...])
    columns = lax.broadcasted_iota(I32, near_scores.shape, 1)
    near_hot = targets[...] - offsets[0] == columns
    far_hot = targets[...] - offsets[1] == columns
    top = jnp.max(jnp.maximum(near_scores, far_scores), axis=1, keepdims=True)
    near_exp = jnp.exp(near_scores - top)
    far_exp = jnp.exp(far_scores - top)
    total = jnp.sum(near_exp + far_exp, axis=1, keepdims=True)
    positive = jnp.sum(
        jnp.where(near_hot, near_scores, 0.0) + jnp.where(far_hot, far_scores, 0.0),
        axis=1,
        keepdims=True,
    )
    grads = dot(jnp.where(near_hot, 0.0, near_exp).astype(BF16), near[...])
    grads = grads + dot(jnp.where(far_hot, 0.0, far_exp).astype(BF16), far[...])
    grads = (grads * (1.0 / total)).astype(BF16)
    pieces = [*split(top + jnp.log(total)), *split(positive)]
    stats = select(lax.broadcasted_iota(I32, (count, 128), 1), pieces).T
    for k in range(count // chunk):
        here = slice(k * chunk, (k + 1) * chunk)
        out[k, :chunk, :] = grads[here]
        out[k, chunk:, :] = jnp.zeros((EXTRA, out.shape[2]), BF16)
        out[k, chunk:, :chunk] = stats[:EXTRA, here].astype(BF16)


def parts_of(offsets, targets, queries, near, far):
    count, width = queries.shape
    return pl.pallas_call(
        parts_kernel,
        out_shape=jax.ShapeDtypeStruct((4, count // 4 + EXTRA, width), BF16),
        in_specs=[SMEM, VMEM, VMEM, VMEM, VMEM],
        out_specs=VMEM,
        compiler_params=PARAMS,
        cost_estimate=pl.CostEstimate(
            flops=8 * count * near.shape[0] * width,
            bytes_accessed=8 * near.shape[0] * width,
            transcendentals=2 * count * near.shape[0],
        ),
    )(offsets, targets, queries, near, far)


def merge_kernel(messages, out, out_logs, out_positive):
    chunk = out.shape[0]
    peers = out_positive.shape[0]
    parts = [messages.at[k] for k in range(messages.shape[0])]
    stats = [part[chunk:, :chunk].astype(F32) for part in parts]
    logs = [stat[0:1] + stat[1:2] + stat[2:3] for stat in stats]
    positive = sum(stat[3:4] + stat[4:5] + stat[5:6] for stat in stats)
    top = logs[0]
    for log in logs[1:]:
        top = jnp.maximum(top, log)
    weights = [jnp.exp(log - top) for log in logs]
    total = sum(weights)
    grads = jnp.zeros(out.shape, F32)
    for part, weight in zip(parts, weights):
        column = jnp.broadcast_to(weight / total, (chunk, chunk)).T[:, :1]
        grads = grads + part[:chunk, :].astype(F32) * column
    out[...] = grads.astype(BF16)
    index = lax.broadcasted_iota(I32, out_logs.shape, 0)
    out_logs[...] = select(index, split(top + jnp.log(total))).astype(BF16)
    peer = lax.broadcasted_iota(I32, (peers, chunk), 0)
    lane = lax.broadcasted_iota(I32, (peers, chunk), 1)
    each = chunk // peers
    own = jnp.zeros((peers, chunk), F32)
    for row in range(each):
        here = lane == peer * each + row
        value = jnp.sum(jnp.where(here, positive, 0.0), axis=1, keepdims=True)
        for k, piece in enumerate(split(value)):
            own = jnp.where(lane == 3 * row + k, piece, own)
    out_positive[...] = own.astype(BF16)


def merge_parts(messages, peers):
    _, rows, width = messages.shape
    chunk = rows - EXTRA
    return pl.pallas_call(
        merge_kernel,
        out_shape=[
            jax.ShapeDtypeStruct((chunk, width), BF16),
            jax.ShapeDtypeStruct((3, chunk), BF16),
            jax.ShapeDtypeStruct((peers, chunk), BF16),
        ],
        in_specs=[VMEM],
        out_specs=[VMEM, VMEM, VMEM],
        compiler_params=PARAMS,
    )(messages)


def final_kernel(places, received, out):
    width = out.shape[2]
    half = received.shape[1] // 2
    column = received.shape[2] - width
    piece = lambda k: received[:, k, width:].astype(F32)
    sums = lambda value: jnp.sum(value, axis=1, keepdims=True)
    logs = piece(0) + piece(1) + piece(2)
    top = jnp.max(logs, axis=0, keepdims=True)
    weights = jnp.exp(logs - top)
    total = jnp.sum(weights, axis=0, keepdims=True)
    log_total = top + jnp.log(total)
    scales = weights / total
    positive = jnp.sum(piece(3), axis=0, keepdims=True)
    lane = lax.broadcasted_iota(I32, (1, column), 1)
    rest = lax.broadcasted_iota(I32, (1, width - column), 1)
    losses = jnp.zeros(rest.shape, F32)
    block = []
    for row in range(half):
        here = lane == places[0] + row
        scale = sums(jnp.where(here, scales, 0.0))
        log_own = sums(jnp.where(here, log_total, 0.0))
        score = sums(jnp.where((lane >= 3 * row) & (lane < 3 * row + 3), positive, 0.0))
        at_positive = (jnp.exp(score - log_own) - 1.0).astype(BF16).astype(F32)
        grads = jnp.sum(received[:, row, :width].astype(F32) * scale, axis=0, keepdims=True)
        positive_row = jnp.sum(received[:, half + row, :width].astype(F32), axis=0, keepdims=True)
        block.append(grads + at_positive * positive_row)
        losses = jnp.where(rest == places[1] + row, log_own - score, losses)
    block.append(jnp.concatenate([log_total, losses], axis=1))
    for k in range(out.shape[0]):
        for row, value in enumerate(block):
            out[k, row : row + 1, :] = value


def final_rows(places, received, width):
    return pl.pallas_call(
        final_kernel,
        out_shape=jax.ShapeDtypeStruct((8, received.shape[1] // 2 + 1, width), F32),
        in_specs=[SMEM, VMEM],
        out_specs=VMEM,
        compiler_params=PARAMS,
    )(places, received)


def passages_kernel(offsets, core, targets, log_totals, passages, own, other, out):
    start = offsets[0] + pl.program_id(0) * passages.shape[0]
    rows = lax.broadcasted_iota(I32, (passages.shape[0], own.shape[0]), 0) + start
    total = None
    for half, queries in enumerate((own, other)):
        first = lax.bitwise_xor(core[0], half) * 4
        row_of = lambda ref: jnp.concatenate([ref[pl.ds(first + k, 1), :] for k in range(4)], axis=1)
        scores = times_t(passages[...], queries[...])
        hot = (row_of(targets) == rows).astype(F32)
        coefficient = (jnp.exp(scores - row_of(log_totals)) - hot).astype(BF16)
        term = dot(coefficient, queries[...])
        total = term if total is None else total + term
    out[...] = total


def passage_grad_of(offsets, core, targets, log_totals, passages, own, other):
    count, width = passages.shape
    step = count // 2
    return pl.pallas_call(
        passages_kernel,
        grid=(count // step,),
        out_shape=jax.ShapeDtypeStruct((count, width), F32),
        in_specs=[
            SMEM,
            SMEM,
            VMEM,
            VMEM,
            pl.BlockSpec((step, width), lambda i: (i, 0)),
            VMEM,
            VMEM,
        ],
        out_specs=pl.BlockSpec((step, width), lambda i: (i, 0)),
        compiler_params=PARAMS,
        cost_estimate=pl.CostEstimate(
            flops=8 * count * own.shape[0] * width,
            bytes_accessed=10 * count * width,
            transcendentals=2 * count * own.shape[0],
        ),
    )(offsets, core, targets, log_totals, passages, own, other)


def order_kernel(high, near, far, out):
    half = out.shape[0] // (2 * near.shape[0])
    for group in range(near.shape[0]):
        mine, other = near[group, :half], far[group, :half]
        low = jnp.where(high[0] == 0, mine, other)
        top = jnp.where(high[0] == 0, other, mine)
        out[2 * half * group : 2 * half * group + half, :] = low
        out[2 * half * group + half : 2 * half * (group + 1), :] = top


def order_rows(high, near, far, half):
    groups, _, width = near.shape
    return pl.pallas_call(
        order_kernel,
        out_shape=jax.ShapeDtypeStruct((2 * half * groups, width), F32),
        in_specs=[SMEM, VMEM, VMEM],
        out_specs=VMEM,
        compiler_params=PARAMS,
    )(high, near, far)


def body(queries, passages, positives):
    rows, width = queries.shape
    passage_count = passages.shape[0]
    blk = lax.axis_size("blk")
    zh = lax.axis_size("zh")
    mine = lax.axis_index("blk")
    y = lax.axis_index("y")
    core = lax.axis_index("c")
    high = lax.axis_index("zh")
    chip = (mine * zh + high) * 4 + y
    part = rows // 8
    column = blk * part
    count = 4 * column

    near, far = passages, swap(passages, "c", 1)
    offsets = jnp.stack([chip * 2 + core, chip * 2 + 1 - core]) * passage_count

    pieces = gather(lax.dynamic_slice_in_dim(queries, (core * 4 + y) * part, part), "blk")

    targets = positives.reshape(blk, 8, part).transpose(1, 0, 2).reshape(8, column)
    own_targets = lax.dynamic_slice_in_dim(targets, core * 4, 4).reshape(count, 1)

    positive_rows = positive_rows_of(offsets, own_targets, near, far).reshape(4, column, width)
    pieces, positive_rows = lax.optimization_barrier((pieces, positive_rows))
    pick = lambda k: lax.dynamic_index_in_dim(positive_rows, lax.bitwise_xor(y, k), 0, keepdims=False)
    positive_parts = [pick(0)] + [swap(pick(k), "y", k) for k in (1, 2, 3)]
    own_queries = gather(pieces.reshape(column, width), "y").reshape(count, width)
    parts = parts_of(offsets, own_targets, own_queries, near, far)
    parts, positive_parts = lax.optimization_barrier((parts, positive_parts))
    positive_rows = sum(v.astype(F32) for v in positive_parts).astype(BF16)
    peers = blk * zh
    half = part // zh
    grads, logs, positive = merge_parts(lax.all_to_all(parts, "y", 0, 0, tiled=True), peers)

    message = jnp.concatenate(
        [grads.reshape(peers, half, width), positive_rows.reshape(peers, half, width)], axis=1
    )
    logs = jnp.broadcast_to(logs[None], (peers,) + logs.shape)
    extra = jnp.concatenate([logs, positive[:, None]], axis=1)
    received = lax.all_to_all(
        jnp.concatenate([message, extra], axis=2), ("blk", "zh"), 0, 0, tiled=True
    )

    other_queries = swap(own_queries, "c", 1)
    received, other_queries = lax.optimization_barrier((received, other_queries))
    places = jnp.stack([mine, core * 4 + y]) * part + high * half
    final = lax.all_to_all(final_rows(places, received, width), ("c", "y"), 0, 0, tiled=True)
    final = lax.optimization_barrier(final)
    far_final = swap(final, "zh", 1)
    log_totals = final[:, half, :column]
    passage_grad = passage_grad_of(
        offsets, core[None], targets, log_totals, passages, own_queries, other_queries
    )
    losses_of = lambda value: jnp.sum(value[:, half, column : column + rows], axis=0)
    query_loss = losses_of(final) + losses_of(far_final)
    query_grad = order_rows(high[None], final, far_final, half)
    return (query_loss, query_grad, passage_grad)


def solution(mesh):
    blk = mesh.shape["blk"]
    narrow = mesh.shape["narrow"]
    fine = Mesh(mesh.devices.reshape(blk, narrow // 8, 4, 2), ("blk", "zh", "y", "c"))
    every = ("blk", "zh", "y", "c")
    return jax.shard_map(
        body,
        mesh=fine,
        in_specs=(P("blk", None), P(every, None), P()),
        out_specs=(P("blk"), P("blk", None), P(every, None)),
        check_vma=False,
    )
```

```python
import jax
import jax.numpy as jnp
from jax import lax
from jax.experimental import pallas as pl
from jax.experimental.pallas import tpu as pltpu
from jax.sharding import Mesh, PartitionSpec as P

F32 = jnp.float32
BF16 = jnp.bfloat16
I32 = jnp.int32
EXTRA = 16
VMEM = pl.BlockSpec(memory_space=pltpu.VMEM)
SMEM = pl.BlockSpec(memory_space=pltpu.SMEM)
PARAMS = pltpu.CompilerParams(vmem_limit_bytes=28 * 1024 * 1024)


def swap(value, axis, offset):
    size = lax.axis_size(axis)
    return lax.ppermute(value, axis, [(i, i ^ offset) for i in range(size)])


def gather(piece, axes):
    size = lax.axis_size(axes)
    return lax.all_to_all(jnp.broadcast_to(piece[None], (size,) + piece.shape), axes, 0, 0, tiled=True)


def times_t(left, right):
    return lax.dot_general(left, right, (((1,), (1,)), ((), ())), preferred_element_type=F32)


def dot(left, right):
    return jnp.dot(left, right, preferred_element_type=F32)


def split(value):
    high = value.astype(BF16).astype(F32)
    rest = value - high
    middle = rest.astype(BF16).astype(F32)
    return high, middle, rest - middle


def select(index, values):
    out = jnp.zeros_like(index, dtype=F32)
    for i, value in enumerate(values):
        out = jnp.where(index == i, value, out)
    return out


def rows_kernel(offsets, targets, near, far, out):
    columns = lax.broadcasted_iota(I32, (targets.shape[0], near.shape[0]), 1)
    near_hot = (targets[...] - offsets[0] == columns).astype(F32).astype(BF16)
    far_hot = (targets[...] - offsets[1] == columns).astype(F32).astype(BF16)
    out[...] = (dot(near_hot, near[...]) + dot(far_hot, far[...])).astype(BF16)


def positive_rows_of(offsets, targets, near, far):
    return pl.pallas_call(
        rows_kernel,
        out_shape=jax.ShapeDtypeStruct((targets.shape[0], near.shape[1]), BF16),
        in_specs=[SMEM, VMEM, VMEM, VMEM],
        out_specs=VMEM,
        compiler_params=PARAMS,
    )(offsets, targets, near, far)


def parts_kernel(offsets, targets, queries, near, far, out):
    chunk = out.shape[1] - EXTRA
    count = queries.shape[0] // 2

    def scores_of(half):
        rows = queries[half * count : (half + 1) * count, :]
        return times_t(rows, near[...]), times_t(rows, far[...])

    following = scores_of(0)
    for half in range(2):
        near_scores, far_scores = following
        if half == 0:
            following = scores_of(1)
        columns = lax.broadcasted_iota(I32, near_scores.shape, 1)
        wanted = targets[half * count : (half + 1) * count, :]
        near_hot = wanted - offsets[0] == columns
        far_hot = wanted - offsets[1] == columns
        top = jnp.max(jnp.maximum(near_scores, far_scores), axis=1, keepdims=True)
        near_exp = jnp.exp(near_scores - top)
        far_exp = jnp.exp(far_scores - top)
        total = jnp.sum(near_exp + far_exp, axis=1, keepdims=True)
        positive = jnp.sum(
            jnp.where(near_hot, near_scores, 0.0) + jnp.where(far_hot, far_scores, 0.0),
            axis=1,
            keepdims=True,
        )
        grads = dot(jnp.where(near_hot, 0.0, near_exp).astype(BF16), near[...])
        grads = grads + dot(jnp.where(far_hot, 0.0, far_exp).astype(BF16), far[...])
        grads = (grads * (1.0 / total)).astype(BF16)
        pieces = [*split(top + jnp.log(total)), *split(positive)]
        stats = select(lax.broadcasted_iota(I32, (count, 128), 1), pieces).T
        for part in range(count // chunk):
            here = slice(part * chunk, (part + 1) * chunk)
            k = half * (count // chunk) + part
            out[k, :chunk, :] = grads[here]
            out[k, chunk:, :] = jnp.zeros((EXTRA, out.shape[2]), BF16)
            out[k, chunk:, :chunk] = stats[:EXTRA, here].astype(BF16)


def parts_of(offsets, targets, queries, near, far):
    count, width = queries.shape
    return pl.pallas_call(
        parts_kernel,
        out_shape=jax.ShapeDtypeStruct((4, count // 4 + EXTRA, width), BF16),
        in_specs=[SMEM, VMEM, VMEM, VMEM, VMEM],
        out_specs=VMEM,
        compiler_params=PARAMS,
        cost_estimate=pl.CostEstimate(
            flops=8 * count * near.shape[0] * width,
            bytes_accessed=8 * near.shape[0] * width,
            transcendentals=2 * count * near.shape[0],
        ),
    )(offsets, targets, queries, near, far)


def merge_kernel(messages, out, out_logs, out_positive):
    chunk = out.shape[0]
    peers = out_positive.shape[0]
    parts = [messages.at[k] for k in range(messages.shape[0])]
    stats = [part[chunk:, :chunk].astype(F32) for part in parts]
    logs = [stat[0:1] + stat[1:2] + stat[2:3] for stat in stats]
    positive = sum(stat[3:4] + stat[4:5] + stat[5:6] for stat in stats)
    top = logs[0]
    for log in logs[1:]:
        top = jnp.maximum(top, log)
    weights = [jnp.exp(log - top) for log in logs]
    total = sum(weights)
    grads = jnp.zeros(out.shape, F32)
    for part, weight in zip(parts, weights):
        column = jnp.broadcast_to(weight / total, (chunk, chunk)).T[:, :1]
        grads = grads + part[:chunk, :].astype(F32) * column
    out[...] = grads.astype(BF16)
    index = lax.broadcasted_iota(I32, out_logs.shape, 0)
    out_logs[...] = select(index, split(top + jnp.log(total))).astype(BF16)
    peer = lax.broadcasted_iota(I32, (peers, chunk), 0)
    lane = lax.broadcasted_iota(I32, (peers, chunk), 1)
    each = chunk // peers
    own = jnp.zeros((peers, chunk), F32)
    for row in range(each):
        here = lane == peer * each + row
        value = jnp.sum(jnp.where(here, positive, 0.0), axis=1, keepdims=True)
        for k, piece in enumerate(split(value)):
            own = jnp.where(lane == 3 * row + k, piece, own)
    out_positive[...] = own.astype(BF16)


def merge_parts(messages, peers):
    _, rows, width = messages.shape
    chunk = rows - EXTRA
    return pl.pallas_call(
        merge_kernel,
        out_shape=[
            jax.ShapeDtypeStruct((chunk, width), BF16),
            jax.ShapeDtypeStruct((3, chunk), BF16),
            jax.ShapeDtypeStruct((peers, chunk), BF16),
        ],
        in_specs=[VMEM],
        out_specs=[VMEM, VMEM, VMEM],
        compiler_params=PARAMS,
    )(messages)


def final_kernel(places, received, out):
    width = out.shape[2]
    half = received.shape[1] // 2
    column = received.shape[2] - width
    piece = lambda k: received[:, k, width:].astype(F32)
    sums = lambda value: jnp.sum(value, axis=1, keepdims=True)
    logs = piece(0) + piece(1) + piece(2)
    top = jnp.max(logs, axis=0, keepdims=True)
    weights = jnp.exp(logs - top)
    total = jnp.sum(weights, axis=0, keepdims=True)
    log_total = top + jnp.log(total)
    scales = weights / total
    positive = jnp.sum(piece(3), axis=0, keepdims=True)
    lane = lax.broadcasted_iota(I32, (1, column), 1)
    rest = lax.broadcasted_iota(I32, (1, width - column), 1)
    losses = jnp.zeros(rest.shape, F32)
    block = []
    for row in range(half):
        here = lane == places[0] + row
        scale = sums(jnp.where(here, scales, 0.0))
        log_own = sums(jnp.where(here, log_total, 0.0))
        score = sums(jnp.where((lane >= 3 * row) & (lane < 3 * row + 3), positive, 0.0))
        at_positive = (jnp.exp(score - log_own) - 1.0).astype(BF16).astype(F32)
        grads = jnp.sum(received[:, row, :width].astype(F32) * scale, axis=0, keepdims=True)
        positive_row = jnp.sum(received[:, half + row, :width].astype(F32), axis=0, keepdims=True)
        block.append(grads + at_positive * positive_row)
        losses = jnp.where(rest == places[1] + row, log_own - score, losses)
    block.append(jnp.concatenate([log_total, losses], axis=1))
    for k in range(out.shape[0]):
        for row, value in enumerate(block):
            out[k, row : row + 1, :] = value


def final_rows(places, received, width):
    return pl.pallas_call(
        final_kernel,
        out_shape=jax.ShapeDtypeStruct((8, received.shape[1] // 2 + 1, width), F32),
        in_specs=[SMEM, VMEM],
        out_specs=VMEM,
        compiler_params=PARAMS,
    )(places, received)


def passages_kernel(offsets, core, targets, log_totals, passages, own, other, out):
    start = offsets[0] + pl.program_id(0) * passages.shape[0]
    rows = lax.broadcasted_iota(I32, (passages.shape[0], own.shape[0]), 0) + start
    total = None
    for half, queries in enumerate((own, other)):
        first = lax.bitwise_xor(core[0], half) * 4
        row_of = lambda ref: jnp.concatenate([ref[pl.ds(first + k, 1), :] for k in range(4)], axis=1)
        scores = times_t(passages[...], queries[...])
        hot = (row_of(targets) == rows).astype(F32)
        coefficient = (jnp.exp(scores - row_of(log_totals)) - hot).astype(BF16)
        term = dot(coefficient, queries[...])
        total = term if total is None else total + term
    out[...] = total


def passage_grad_of(offsets, core, targets, log_totals, passages, own, other):
    count, width = passages.shape
    step = count // 2
    return pl.pallas_call(
        passages_kernel,
        grid=(count // step,),
        out_shape=jax.ShapeDtypeStruct((count, width), F32),
        in_specs=[
            SMEM,
            SMEM,
            VMEM,
            VMEM,
            pl.BlockSpec((step, width), lambda i: (i, 0)),
            VMEM,
            VMEM,
        ],
        out_specs=pl.BlockSpec((step, width), lambda i: (i, 0)),
        compiler_params=PARAMS,
        cost_estimate=pl.CostEstimate(
            flops=8 * count * own.shape[0] * width,
            bytes_accessed=10 * count * width,
            transcendentals=2 * count * own.shape[0],
        ),
    )(offsets, core, targets, log_totals, passages, own, other)


def order_kernel(high, near, far, out, out_losses):
    half = out.shape[0] // (2 * near.shape[0])
    for group in range(near.shape[0]):
        mine, other = near[group, :half], far[group, :half]
        low = jnp.where(high[0] == 0, mine, other)
        top = jnp.where(high[0] == 0, other, mine)
        out[2 * half * group : 2 * half * group + half, :] = low
        out[2 * half * group + half : 2 * half * (group + 1), :] = top
    losses = jnp.zeros(out_losses.shape, F32)
    for group in range(near.shape[0]):
        for value in (near, far):
            losses = losses + value[group, half : half + 1, near.shape[2] - losses.shape[1] :]
    out_losses[...] = losses


def order_rows(high, near, far, half, first):
    groups, _, width = near.shape
    return pl.pallas_call(
        order_kernel,
        out_shape=[
            jax.ShapeDtypeStruct((2 * half * groups, width), F32),
            jax.ShapeDtypeStruct((1, width - first), F32),
        ],
        in_specs=[SMEM, VMEM, VMEM],
        out_specs=[VMEM, VMEM],
        compiler_params=PARAMS,
    )(high, near, far)


def body(queries, passages, positives):
    rows, width = queries.shape
    passage_count = passages.shape[0]
    blk = lax.axis_size("blk")
    zh = lax.axis_size("zh")
    mine = lax.axis_index("blk")
    y = lax.axis_index("y")
    core = lax.axis_index("c")
    high = lax.axis_index("zh")
    chip = (mine * zh + high) * 4 + y
    part = rows // 8
    column = blk * part
    count = 4 * column

    near, far = passages, swap(passages, "c", 1)
    offsets = jnp.stack([chip * 2 + core, chip * 2 + 1 - core]) * passage_count

    pieces = gather(lax.dynamic_slice_in_dim(queries, (core * 4 + y) * part, part), "blk")

    targets = positives.reshape(blk, 8, part).transpose(1, 0, 2).reshape(8, column)
    own_targets = lax.dynamic_slice_in_dim(targets, core * 4, 4).reshape(count, 1)

    positive_rows = positive_rows_of(offsets, own_targets, near, far).reshape(4, column, width)
    pieces, positive_rows = lax.optimization_barrier((pieces, positive_rows))
    pick = lambda k: lax.dynamic_index_in_dim(positive_rows, lax.bitwise_xor(y, k), 0, keepdims=False)
    positive_parts = [pick(0)] + [swap(pick(k), "y", k) for k in (1, 2, 3)]
    own_queries = gather(pieces.reshape(column, width), "y").reshape(count, width)
    parts = parts_of(offsets, own_targets, own_queries, near, far)
    parts, positive_parts = lax.optimization_barrier((parts, positive_parts))
    positive_rows = sum(v.astype(F32) for v in positive_parts).astype(BF16)
    peers = blk * zh
    half = part // zh
    grads, logs, positive = merge_parts(lax.all_to_all(parts, "y", 0, 0, tiled=True), peers)

    message = jnp.concatenate(
        [grads.reshape(peers, half, width), positive_rows.reshape(peers, half, width)], axis=1
    )
    logs = jnp.broadcast_to(logs[None], (peers,) + logs.shape)
    extra = jnp.concatenate([logs, positive[:, None]], axis=1)
    received = lax.all_to_all(
        jnp.concatenate([message, extra], axis=2), ("blk", "zh"), 0, 0, tiled=True
    )

    other_queries = swap(own_queries, "c", 1)
    received, other_queries = lax.optimization_barrier((received, other_queries))
    places = jnp.stack([mine, core * 4 + y]) * part + high * half
    final = lax.all_to_all(final_rows(places, received, width), ("c", "y"), 0, 0, tiled=True)
    final = lax.optimization_barrier(final)
    far_final = swap(final, "zh", 1)
    log_totals = final[:, half, :column]
    passage_grad = passage_grad_of(
        offsets, core[None], targets, log_totals, passages, own_queries, other_queries
    )
    query_grad, losses = order_rows(high[None], final, far_final, half, column)
    query_loss = losses[0, :rows]
    return (query_loss, query_grad, passage_grad)


def solution(mesh):
    blk = mesh.shape["blk"]
    narrow = mesh.shape["narrow"]
    fine = Mesh(mesh.devices.reshape(blk, narrow // 8, 4, 2), ("blk", "zh", "y", "c"))
    every = ("blk", "zh", "y", "c")
    return jax.shard_map(
        body,
        mesh=fine,
        in_specs=(P("blk", None), P(every, None), P()),
        out_specs=(P("blk"), P("blk", None), P(every, None)),
        check_vma=False,
    )
```

```python
import jax
import jax.numpy as jnp
from jax import lax
from jax.experimental import pallas as pl
from jax.experimental.pallas import tpu as pltpu
from jax.sharding import Mesh, PartitionSpec as P

F32 = jnp.float32
BF16 = jnp.bfloat16
I32 = jnp.int32
EXTRA = 16
VMEM = pl.BlockSpec(memory_space=pltpu.VMEM)
SMEM = pl.BlockSpec(memory_space=pltpu.SMEM)
PARAMS = pltpu.CompilerParams(vmem_limit_bytes=28 * 1024 * 1024)


def swap(value, axis, offset):
    size = lax.axis_size(axis)
    return lax.ppermute(value, axis, [(i, i ^ offset) for i in range(size)])


def gather(piece, axes):
    size = lax.axis_size(axes)
    return lax.all_to_all(jnp.broadcast_to(piece[None], (size,) + piece.shape), axes, 0, 0, tiled=True)


def times_t(left, right):
    return lax.dot_general(left, right, (((1,), (1,)), ((), ())), preferred_element_type=F32)


def dot(left, right):
    return jnp.dot(left, right, preferred_element_type=F32)


def split(value):
    high = value.astype(BF16).astype(F32)
    rest = value - high
    middle = rest.astype(BF16).astype(F32)
    return high, middle, rest - middle


def select(index, values):
    out = jnp.zeros_like(index, dtype=F32)
    for i, value in enumerate(values):
        out = jnp.where(index == i, value, out)
    return out


def rows_kernel(offsets, targets, near, far, out):
    columns = lax.broadcasted_iota(I32, (targets.shape[0], near.shape[0]), 1)
    near_hot = (targets[...] - offsets[0] == columns).astype(F32).astype(BF16)
    far_hot = (targets[...] - offsets[1] == columns).astype(F32).astype(BF16)
    out[...] = (dot(near_hot, near[...]) + dot(far_hot, far[...])).astype(BF16)


def positive_rows_of(offsets, targets, near, far):
    return pl.pallas_call(
        rows_kernel,
        out_shape=jax.ShapeDtypeStruct((targets.shape[0], near.shape[1]), BF16),
        in_specs=[SMEM, VMEM, VMEM, VMEM],
        out_specs=VMEM,
        compiler_params=PARAMS,
    )(offsets, targets, near, far)


def parts_kernel(offsets, targets, queries, near, far, out):
    chunk = out.shape[1] - EXTRA
    count = queries.shape[0] // 2

    def scores_of(half):
        rows = queries[half * count : (half + 1) * count, :]
        return times_t(rows, near[...]), times_t(rows, far[...])

    following = scores_of(0)
    for half in range(2):
        near_scores, far_scores = following
        if half == 0:
            following = scores_of(1)
        columns = lax.broadcasted_iota(I32, near_scores.shape, 1)
        wanted = targets[half * count : (half + 1) * count, :]
        near_hot = wanted - offsets[0] == columns
        far_hot = wanted - offsets[1] == columns
        top = jnp.max(jnp.maximum(near_scores, far_scores), axis=1, keepdims=True)
        near_exp = jnp.exp(near_scores - top)
        far_exp = jnp.exp(far_scores - top)
        total = jnp.sum(near_exp + far_exp, axis=1, keepdims=True)
        positive = jnp.sum(
            jnp.where(near_hot, near_scores, 0.0) + jnp.where(far_hot, far_scores, 0.0),
            axis=1,
            keepdims=True,
        )
        grads = dot(jnp.where(near_hot, 0.0, near_exp).astype(BF16), near[...])
        grads = grads + dot(jnp.where(far_hot, 0.0, far_exp).astype(BF16), far[...])
        grads = (grads * (1.0 / total)).astype(BF16)
        pieces = [*split(top + jnp.log(total)), *split(positive)]
        stats = select(lax.broadcasted_iota(I32, (count, 128), 1), pieces).T
        for part in range(count // chunk):
            here = slice(part * chunk, (part + 1) * chunk)
            k = half * (count // chunk) + part
            out[k, :chunk, :] = grads[here]
            out[k, chunk:, :] = jnp.zeros((EXTRA, out.shape[2]), BF16)
            out[k, chunk:, :chunk] = stats[:EXTRA, here].astype(BF16)


def parts_of(offsets, targets, queries, near, far):
    count, width = queries.shape
    return pl.pallas_call(
        parts_kernel,
        out_shape=jax.ShapeDtypeStruct((4, count // 4 + EXTRA, width), BF16),
        in_specs=[SMEM, VMEM, VMEM, VMEM, VMEM],
        out_specs=VMEM,
        compiler_params=PARAMS,
        cost_estimate=pl.CostEstimate(
            flops=8 * count * near.shape[0] * width,
            bytes_accessed=8 * near.shape[0] * width,
            transcendentals=2 * count * near.shape[0],
        ),
    )(offsets, targets, queries, near, far)


def merge_kernel(messages, out, out_logs, out_positive):
    chunk = out.shape[0]
    peers = out_positive.shape[0]
    parts = [messages.at[k] for k in range(messages.shape[0])]
    stats = [part[chunk:, :chunk].astype(F32) for part in parts]
    logs = [stat[0:1] + stat[1:2] + stat[2:3] for stat in stats]
    positive = sum(stat[3:4] + stat[4:5] + stat[5:6] for stat in stats)
    top = logs[0]
    for log in logs[1:]:
        top = jnp.maximum(top, log)
    weights = [jnp.exp(log - top) for log in logs]
    total = sum(weights)
    grads = jnp.zeros(out.shape, F32)
    for part, weight in zip(parts, weights):
        column = jnp.broadcast_to(weight / total, (chunk, chunk)).T[:, :1]
        grads = grads + part[:chunk, :].astype(F32) * column
    out[...] = grads.astype(BF16)
    index = lax.broadcasted_iota(I32, out_logs.shape, 0)
    out_logs[...] = select(index, split(top + jnp.log(total))).astype(BF16)
    peer = lax.broadcasted_iota(I32, (peers, chunk), 0)
    lane = lax.broadcasted_iota(I32, (peers, chunk), 1)
    each = chunk // peers
    own = jnp.zeros((peers, chunk), F32)
    for row in range(each):
        here = lane == peer * each + row
        value = jnp.sum(jnp.where(here, positive, 0.0), axis=1, keepdims=True)
        for k, piece in enumerate(split(value)):
            own = jnp.where(lane == 3 * row + k, piece, own)
    out_positive[...] = own.astype(BF16)


def merge_parts(messages, peers):
    _, rows, width = messages.shape
    chunk = rows - EXTRA
    return pl.pallas_call(
        merge_kernel,
        out_shape=[
            jax.ShapeDtypeStruct((chunk, width), BF16),
            jax.ShapeDtypeStruct((3, chunk), BF16),
            jax.ShapeDtypeStruct((peers, chunk), BF16),
        ],
        in_specs=[VMEM],
        out_specs=[VMEM, VMEM, VMEM],
        compiler_params=PARAMS,
    )(messages)


def final_kernel(places, received, out):
    width = out.shape[2]
    half = received.shape[1] // 2
    column = received.shape[2] - width
    piece = lambda k: received[:, k, width:].astype(F32)
    sums = lambda value: jnp.sum(value, axis=1, keepdims=True)
    logs = piece(0) + piece(1) + piece(2)
    top = jnp.max(logs, axis=0, keepdims=True)
    weights = jnp.exp(logs - top)
    total = jnp.sum(weights, axis=0, keepdims=True)
    log_total = top + jnp.log(total)
    scales = weights / total
    positive = jnp.sum(piece(3), axis=0, keepdims=True)
    lane = lax.broadcasted_iota(I32, (1, column), 1)
    rest = lax.broadcasted_iota(I32, (1, width - column), 1)
    losses = jnp.zeros(rest.shape, F32)
    block = []
    for row in range(half):
        here = lane == places[0] + row
        scale = sums(jnp.where(here, scales, 0.0))
        log_own = sums(jnp.where(here, log_total, 0.0))
        score = sums(jnp.where((lane >= 3 * row) & (lane < 3 * row + 3), positive, 0.0))
        at_positive = (jnp.exp(score - log_own) - 1.0).astype(BF16).astype(F32)
        grads = jnp.sum(received[:, row, :width].astype(F32) * scale, axis=0, keepdims=True)
        positive_row = jnp.sum(received[:, half + row, :width].astype(F32), axis=0, keepdims=True)
        block.append(grads + at_positive * positive_row)
        losses = jnp.where(rest == places[1] + row, log_own - score, losses)
    block.append(jnp.concatenate([log_total, losses], axis=1))
    for k in range(out.shape[0]):
        for row, value in enumerate(block):
            out[k, row : row + 1, :] = value


def final_rows(places, received, width):
    return pl.pallas_call(
        final_kernel,
        out_shape=jax.ShapeDtypeStruct((8, received.shape[1] // 2 + 1, width), F32),
        in_specs=[SMEM, VMEM],
        out_specs=VMEM,
        compiler_params=PARAMS,
    )(places, received)


def passages_kernel(offsets, core, targets, log_totals, passages, own, other, out):
    start = offsets[0] + pl.program_id(0) * passages.shape[0]
    rows = lax.broadcasted_iota(I32, (passages.shape[0], own.shape[0]), 0) + start
    total = None
    for half, queries in enumerate((own, other)):
        first = lax.bitwise_xor(core[0], half) * 4
        row_of = lambda ref: jnp.concatenate([ref[pl.ds(first + k, 1), :] for k in range(4)], axis=1)
        scores = times_t(passages[...], queries[...])
        hot = (row_of(targets) == rows).astype(F32)
        coefficient = (jnp.exp(scores - row_of(log_totals)) - hot).astype(BF16)
        term = dot(coefficient, queries[...])
        total = term if total is None else total + term
    out[...] = total


def passage_grad_of(offsets, core, targets, log_totals, passages, own, other):
    count, width = passages.shape
    step = count // 2
    return pl.pallas_call(
        passages_kernel,
        grid=(count // step,),
        out_shape=jax.ShapeDtypeStruct((count, width), F32),
        in_specs=[
            SMEM,
            SMEM,
            VMEM,
            VMEM,
            pl.BlockSpec((step, width), lambda i: (i, 0)),
            VMEM,
            VMEM,
        ],
        out_specs=pl.BlockSpec((step, width), lambda i: (i, 0)),
        compiler_params=PARAMS,
        cost_estimate=pl.CostEstimate(
            flops=8 * count * own.shape[0] * width,
            bytes_accessed=10 * count * width,
            transcendentals=2 * count * own.shape[0],
        ),
    )(offsets, core, targets, log_totals, passages, own, other)


def order_kernel(high, near, far, out, out_losses):
    half = out.shape[0] // (2 * near.shape[0])
    for group in range(near.shape[0]):
        mine, other = near[group, :half], far[group, :half]
        low = jnp.where(high[0] == 0, mine, other)
        top = jnp.where(high[0] == 0, other, mine)
        out[2 * half * group : 2 * half * group + half, :] = low
        out[2 * half * group + half : 2 * half * (group + 1), :] = top
    losses = jnp.zeros(out_losses.shape, F32)
    for group in range(near.shape[0]):
        for value in (near, far):
            losses = losses + value[group, half : half + 1, near.shape[2] - losses.shape[1] :]
    out_losses[...] = losses


def order_rows(high, near, far, half, first):
    groups, _, width = near.shape
    return pl.pallas_call(
        order_kernel,
        out_shape=[
            jax.ShapeDtypeStruct((2 * half * groups, width), F32),
            jax.ShapeDtypeStruct((1, width - first), F32),
        ],
        in_specs=[SMEM, VMEM, VMEM],
        out_specs=[VMEM, VMEM],
        compiler_params=PARAMS,
    )(high, near, far)


def body(queries, passages, positives):
    rows, width = queries.shape
    passage_count = passages.shape[0]
    blk = lax.axis_size("blk")
    zh = lax.axis_size("zh")
    mine = lax.axis_index("blk")
    y = lax.axis_index("y")
    core = lax.axis_index("c")
    high = lax.axis_index("zh")
    chip = (mine * zh + high) * 4 + y
    part = rows // 8
    column = blk * part
    count = 4 * column

    near, far = passages, swap(passages, "c", 1)
    offsets = jnp.stack([chip * 2 + core, chip * 2 + 1 - core]) * passage_count

    pieces = gather(lax.dynamic_slice_in_dim(queries, (core * 4 + y) * part, part), "blk")

    targets = positives.reshape(blk, 8, part).transpose(1, 0, 2).reshape(8, column)
    own_targets = lax.dynamic_slice_in_dim(targets, core * 4, 4).reshape(count, 1)

    positive_rows = positive_rows_of(offsets, own_targets, near, far).reshape(4, column, width)
    pieces, positive_rows = lax.optimization_barrier((pieces, positive_rows))
    pick = lambda k: lax.dynamic_index_in_dim(positive_rows, lax.bitwise_xor(y, k), 0, keepdims=False)
    positive_parts = [pick(0)] + [swap(pick(k), "y", k) for k in (1, 2, 3)]
    pieces, positive_parts = lax.optimization_barrier((pieces, positive_parts))
    own_queries = gather(pieces.reshape(column, width), "y").reshape(count, width)
    parts = parts_of(offsets, own_targets, own_queries, near, far)
    parts, positive_parts = lax.optimization_barrier((parts, positive_parts))
    positive_rows = sum(v.astype(F32) for v in positive_parts).astype(BF16)
    peers = blk * zh
    half = part // zh
    grads, logs, positive = merge_parts(lax.all_to_all(parts, "y", 0, 0, tiled=True), peers)

    message = jnp.concatenate(
        [grads.reshape(peers, half, width), positive_rows.reshape(peers, half, width)], axis=1
    )
    logs = jnp.broadcast_to(logs[None], (peers,) + logs.shape)
    extra = jnp.concatenate([logs, positive[:, None]], axis=1)
    received = lax.all_to_all(
        jnp.concatenate([message, extra], axis=2), ("blk", "zh"), 0, 0, tiled=True
    )

    other_queries = swap(own_queries, "c", 1)
    received, other_queries = lax.optimization_barrier((received, other_queries))
    places = jnp.stack([mine, core * 4 + y]) * part + high * half
    final = lax.all_to_all(final_rows(places, received, width), ("c", "y"), 0, 0, tiled=True)
    final = lax.optimization_barrier(final)
    far_final = swap(final, "zh", 1)
    log_totals = final[:, half, :column]
    passage_grad = passage_grad_of(
        offsets, core[None], targets, log_totals, passages, own_queries, other_queries
    )
    query_grad, losses = order_rows(high[None], final, far_final, half, column)
    query_loss = losses[0, :rows]
    return (query_loss, query_grad, passage_grad)


def solution(mesh):
    blk = mesh.shape["blk"]
    narrow = mesh.shape["narrow"]
    fine = Mesh(mesh.devices.reshape(blk, narrow // 8, 4, 2), ("blk", "zh", "y", "c"))
    every = ("blk", "zh", "y", "c")
    return jax.shard_map(
        body,
        mesh=fine,
        in_specs=(P("blk", None), P(every, None), P()),
        out_specs=(P("blk"), P("blk", None), P(every, None)),
        check_vma=False,
    )
```
